32 devices in a mesh: dp: 8 (over y, x, core), group: 4 (over z).
Axes of the slice: x: 2, y: 2, z: 4, core: 2. Of those that a mesh axis runs over, the one named last changes fastest.
Arguments:
- tokens: float32 [6304, 768], P(('dp', 'group')), may hold values from -6 to 6
- cotangent: float32 [6304, 768], P(('dp', 'group')), may hold values from -6 to 6
- expert_ids: int32 [6304, 2], P(('dp', 'group')), may hold values from 0 to 15, as said below
- slot_pos: int32 [6304, 2], P(('dp', 'group')), may hold values from -1 to 24, as said below
- qkv_w: float32 [768, 2304], P(('dp', 'group')), may hold values from -0.21875 to 0.21875
- qkv_m: float32 [768, 2304], P(('dp', 'group')), may hold values from -18 to 18
- qkv_v: float32 [768, 2304], P(('dp', 'group')), may hold values from 0.3 to 3
- out_w: float32 [768, 768], P(('dp', 'group')), may hold values from -0.875 to 0.875
- out_m: float32 [768, 768], P(('dp', 'group')), may hold values from -18 to 18
- out_v: float32 [768, 768], P(('dp', 'group')), may hold values from 0.3 to 3
- vectors: float32 [39, 768], P(None, ('dp', 'group'))
- vec_m: float32 [39, 768], P(None, ('dp', 'group')), may hold values from -120 to 120
- vec_v: float32 [39, 768], P(None, ('dp', 'group')), may hold values from 40 to 4000
- w_in: float32 [768, 49152], P('group', 'dp'), may hold values from -0.21875 to 0.21875
- w_in_m: float32 [768, 49152], P('group', 'dp'), may hold values from -15 to 15
- w_in_v: float32 [768, 49152], P('group', 'dp'), may hold values from 0.17 to 1.7
- w_out: float32 [49152, 768], P('dp', 'group'), may hold values from -0.875 to 0.875
- w_out_m: float32 [49152, 768], P('dp', 'group'), may hold values from -4 to 4
- w_out_v: float32 [49152, 768], P('dp', 'group'), may hold values from 0.01 to 0.1
- b_in: float32 [49152], P(('dp', 'group')), may hold values from -3 to 3
- b_in_m: float32 [49152], P(('dp', 'group')), may hold values from -15 to 15
- b_in_v: float32 [49152], P(('dp', 'group')), may hold values from 0.17 to 1.7
Outputs:
- block_out: float32 [6304, 768], P(('dp', 'group'))
- input_grad: float32 [6304, 768], P(('dp', 'group'))
- qkv_grad: float32 [768, 2304], P(('dp', 'group'))
- qkv_new: float32 [768, 2304], P(('dp', 'group'))
- qkv_m_new: float32 [768, 2304], P(('dp', 'group'))
- qkv_v_new: float32 [768, 2304], P(('dp', 'group'))
- out_grad: float32 [768, 768], P(('dp', 'group'))
- out_new: float32 [768, 768], P(('dp', 'group'))
- out_m_new: float32 [768, 768], P(('dp', 'group'))
- out_v_new: float32 [768, 768], P(('dp', 'group'))
- vec_grad: float32 [39, 768], P(None, ('dp', 'group'))
- vec_new: float32 [39, 768], P(None, ('dp', 'group'))
- vec_m_new: float32 [39, 768], P(None, ('dp', 'group'))
- vec_v_new: float32 [39, 768], P(None, ('dp', 'group'))
- w_in_grad: float32 [768, 49152], P('group', 'dp')
- w_in_new: float32 [768, 49152], P('group', 'dp')
- w_in_m_new: float32 [768, 49152], P('group', 'dp')
- w_in_v_new: float32 [768, 49152], P('group', 'dp')
- w_out_grad: float32 [49152, 768], P('dp', 'group')
- w_out_new: float32 [49152, 768], P('dp', 'group')
- w_out_m_new: float32 [49152, 768], P('dp', 'group')
- w_out_v_new: float32 [49152, 768], P('dp', 'group')
- b_in_grad: float32 [49152], P(('dp', 'group'))
- b_in_new: float32 [49152], P(('dp', 'group'))
- b_in_m_new: float32 [49152], P(('dp', 'group'))
- b_in_v_new: float32 [49152], P(('dp', 'group'))
- branch_bias_grad: float32 [17, 768], P(None, ('dp', 'group'))
The draws below stay inside these ranges and needn't reach their ends.
Inputs may be any that keep to these rules, and one draw needn't show every extreme that they name: `expert_ids`: each row names two different experts. `slot_pos`: the slot of a choice in its expert's buffer for its aligned block of 197 rows; slots of one expert within a block are distinct; -1 marks a dropped choice; in every block some expert fills all 25 slots.
All inputs are finite; a program needn't handle non-finite values.
Results may differ from the reference program's by a relative error of at most 0.018.
Values may be sent and summed in bfloat16 or wider, within the bound.
No kernel may reach another device: no remote copies, remote signals or barrier semaphores. Data moves between devices by JAX's collectives and lax.ppermute only.
A program may use at most 256 MiB of HBM per device.

```python
import math
import jax
import jax.numpy as jnp
from jax import lax

D = 768
HEADS = 12
HEAD = 64
FF = 3072
EXPERTS = 16
SEQ = 197
TOK_DEV = 197
TOKENS = 6304
CAP = 25
NVEC = 39


def routing_draw(key):
    blocks = TOKENS // TOK_DEV
    key_first, key_second, key_hot, key_order = jax.random.split(jax.random.fold_in(key, 11), 4)
    first_pick = jax.random.randint(key_first, (blocks, TOK_DEV), 0, EXPERTS, dtype=jnp.int32)
    step_pick = jax.random.randint(key_second, (blocks, TOK_DEV), 1, EXPERTS, dtype=jnp.int32)
    hot_expert = jax.random.randint(key_hot, (blocks, 1), 0, EXPERTS, dtype=jnp.int32)
    order_score = jax.random.randint(key_order, (blocks, TOK_DEV), 0, 1 << 20, dtype=jnp.int32) * TOK_DEV
    order_score = order_score + jnp.arange(TOK_DEV, dtype=jnp.int32)[None, :]
    priority = jnp.argsort(jnp.argsort(order_score, axis=1), axis=1).astype(jnp.int32)
    first_pick = jnp.where(priority < CAP, hot_expert, first_pick)
    second_pick = (first_pick + step_pick) % EXPERTS
    picked_pair = jnp.stack([first_pick, second_pick], axis=-1)
    rank_key = priority[..., None] * 2 + jnp.arange(2, dtype=jnp.int32)[None, None, :]
    flat_experts = picked_pair.reshape(blocks, 2 * TOK_DEV)
    flat_rank = rank_key.reshape(blocks, 2 * TOK_DEV)
    order_index = jnp.argsort(flat_rank, axis=1)
    sorted_experts = jnp.take_along_axis(flat_experts, order_index, axis=1)
    onehot_int = (sorted_experts[..., None] == jnp.arange(EXPERTS, dtype=jnp.int32)[None, None, :]).astype(jnp.int32)
    before = jnp.cumsum(onehot_int, axis=1) - onehot_int
    rank_sorted = jnp.sum(before * onehot_int, axis=-1)
    rank_flat = jnp.take_along_axis(rank_sorted, jnp.argsort(order_index, axis=1), axis=1)
    slot_values = jnp.where(rank_flat < CAP, rank_flat, -1)
    return (picked_pair.reshape(TOKENS, 2).astype(jnp.int32), slot_values.reshape(TOKENS, 2).astype(jnp.int32))


def draw_expert_ids(key, part):
    return routing_draw(key)[0]


def draw_slot_pos(key, part):
    return routing_draw(key)[1]


def draw_vectors(key, part):
    noise_draw = jax.random.normal(key, (NVEC, D), jnp.float32)
    row_index = jnp.arange(NVEC)[:, None]
    head_scales = jnp.array([0.1, 0.3, 0.1, 0.3, 0.5, 0.5, 0.3], jnp.float32)
    row_scale = jnp.where(row_index < 7, head_scales[jnp.minimum(row_index, 6)], jnp.where(row_index < 7 + EXPERTS, 2.0 / math.sqrt(D), 0.3))
    offset = jnp.where((row_index == 0) | (row_index == 2), 1.0, 0.0)
    return offset + row_scale * noise_draw


def block_levels(stream_key, dims, cuts, low, high):
    factor_of, own = 1.0, jax.random.fold_in(stream_key, 6)
    for position, parts in cuts:
        heights = jnp.exp(jax.random.uniform(jax.random.fold_in(own, position), (parts,), jnp.float32, low / len(cuts), high / len(cuts)))
        factor_of = factor_of * jnp.repeat(heights, dims[position] // parts).reshape([-1 if axis == position else 1 for axis in range(len(dims))])
    return factor_of


def gaussian(key, shape, scale, limit, cuts=(), kind=jnp.bfloat16):
    values = scale * jax.random.normal(key, shape, jnp.float32)
    if cuts:
        values = values * block_levels(key, shape, cuts, -0.22, 0.18)
    return jnp.clip(values, -limit, limit).astype(kind)


def setup_inputs(seed: int = 0) -> dict:
    key_list = jax.random.split(jax.random.key(seed), 23)
    tokens = gaussian(key_list[0], (TOKENS, D), 1.0, 6.0, ((0, 32),), jnp.float32)
    cotangent = gaussian(key_list[1], (TOKENS, D), 1.0, 6.0, ((0, 32),), jnp.float32)
    expert_ids = draw_expert_ids(jax.random.fold_in(key_list[22], 71), 0)
    slot_pos = draw_slot_pos(jax.random.fold_in(key_list[22], 71), 0)
    qkv_w = gaussian(key_list[4], (D, 3 * D), D ** -0.5, 0.21875, ((0, 32),), jnp.float32)
    qkv_m = gaussian(key_list[5], (D, 3 * D), 3.0, 18.0, ((0, 32),), jnp.float32)
    qkv_v = jnp.clip(jnp.exp(math.log(3.0) - 2.3025851 * jax.random.uniform(key_list[6], (D, 3 * D), jnp.float32) ** block_levels(key_list[6], (D, 3 * D), ((0, 32),), -0.2, 0.2)), 0.3, 3.0)
    out_w = gaussian(key_list[7], (D, D), (D // 16) ** -0.5, 0.875, ((0, 32),), jnp.float32)
    out_m = gaussian(key_list[8], (D, D), 3.0, 18.0, ((0, 32),), jnp.float32)
    out_v = jnp.clip(jnp.exp(math.log(3.0) - 2.3025851 * jax.random.uniform(key_list[9], (D, D), jnp.float32) ** block_levels(key_list[9], (D, D), ((0, 32),), -0.2, 0.2)), 0.3, 3.0)
    vectors = draw_vectors(jax.random.fold_in(key_list[22], 71), 0)
    vec_m = gaussian(key_list[11], (NVEC, D), 20.0, 120.0, ((1, 32),), jnp.float32)
    vec_v = jnp.clip(jnp.exp(math.log(4000.0) - 4.6051702 * jax.random.uniform(key_list[12], (NVEC, D), jnp.float32) ** block_levels(key_list[12], (NVEC, D), ((1, 32),), -0.2, 0.2)), 40.0, 4000.0)
    w_in = gaussian(key_list[13], (D, EXPERTS * FF), D ** -0.5, 0.21875, ((0, 4), (1, 8)), jnp.float32)
    w_in_m = gaussian(key_list[14], (D, EXPERTS * FF), 2.4, 15.0, ((0, 4), (1, 8)), jnp.float32)
    w_in_v = jnp.clip(jnp.exp(math.log(1.7) - 2.3025851 * jax.random.uniform(key_list[15], (D, EXPERTS * FF), jnp.float32) ** block_levels(key_list[15], (D, EXPERTS * FF), ((0, 4), (1, 8)), -0.2, 0.2)), 0.17, 1.7)
    w_out = gaussian(key_list[16], (EXPERTS * FF, D), (FF // 64) ** -0.5, 0.875, ((0, 8), (1, 4)), jnp.float32)
    w_out_m = gaussian(key_list[17], (EXPERTS * FF, D), 0.6, 4.0, ((0, 8), (1, 4)), jnp.float32)
    w_out_v = jnp.clip(jnp.exp(math.log(0.1) - 2.3025851 * jax.random.uniform(key_list[18], (EXPERTS * FF, D), jnp.float32) ** block_levels(key_list[18], (EXPERTS * FF, D), ((0, 8), (1, 4)), -0.2, 0.2)), 0.01, 0.1)
    b_in = gaussian(key_list[19], (EXPERTS * FF,), 0.5, 3.0, ((0, 32),), jnp.float32)
    b_in_m = gaussian(key_list[20], (EXPERTS * FF,), 2.4, 15.0, ((0, 32),), jnp.float32)
    b_in_v = jnp.clip(jnp.exp(math.log(1.7) - 2.3025851 * jax.random.uniform(key_list[21], (EXPERTS * FF,), jnp.float32) ** block_levels(key_list[21], (EXPERTS * FF,), ((0, 32),), -0.2, 0.2)), 0.17, 1.7)
    return dict(tokens=tokens, cotangent=cotangent, expert_ids=expert_ids, slot_pos=slot_pos, qkv_w=qkv_w, qkv_m=qkv_m, qkv_v=qkv_v, out_w=out_w, out_m=out_m, out_v=out_v, vectors=vectors, vec_m=vec_m, vec_v=vec_v, w_in=w_in, w_in_m=w_in_m, w_in_v=w_in_v, w_out=w_out, w_out_m=w_out_m, w_out_v=w_out_v, b_in=b_in, b_in_m=b_in_m, b_in_v=b_in_v)


LEARN_RATE = 0.15
BETA_ONE = 0.9
BETA_TWO = 0.999
ADAM_EPS = 1e-08
WEIGHT_DECAY = 0.1
CORR_ONE = 1.0 - BETA_ONE ** 2
CORR_TWO = 1.0 - BETA_TWO ** 2
NORM_EPS = 1e-06
EXACT = lax.Precision.HIGHEST

def to_half(values):
    return values.astype(jnp.bfloat16)

def heads_view(values):
    return values.reshape(-1, SEQ, HEADS, HEAD).astype(jnp.float32)

def normalize(values):
    average = lax.optimization_barrier(jnp.mean(values, axis=-1, keepdims=True))
    centered = values - average
    inv_std = lax.rsqrt(lax.optimization_barrier(jnp.mean(centered * centered, axis=-1, keepdims=True)) + NORM_EPS)
    return (centered * inv_std, inv_std)

def normalize_back(grad_norm, normed, inv_std):
    return inv_std * (grad_norm - lax.optimization_barrier(jnp.mean(grad_norm, axis=-1, keepdims=True)) - normed * lax.optimization_barrier(jnp.mean(grad_norm * normed, axis=-1, keepdims=True)))

def expert_table(ids_here):
    return (ids_here[..., None] == jnp.arange(EXPERTS)[None, None, :]).astype(jnp.float32)

def slot_table(ids_here, slots_here):
    kept_mask = slots_here >= 0
    target = ids_here * CAP + slots_here
    slot_hits = (target[..., None] == jnp.arange(EXPERTS * CAP)[None, None, :]) & kept_mask[..., None]
    return (slot_hits.astype(jnp.float32), kept_mask)

def select_rows(results, ids_here, slots_here):
    kept_mask = slots_here >= 0
    flat_index = jnp.where(kept_mask, ids_here * CAP + slots_here, 0)
    return (jnp.take(results, flat_index, axis=0), kept_mask)

def forward_rows(row_block, qkv_half, out_half, vec_real, router_half):
    normed_one, inv_one = normalize(row_block)
    attn_in = to_half(normed_one * vec_real[0] + vec_real[1])
    projected = jnp.dot(attn_in, qkv_half, preferred_element_type=jnp.float32)
    queries = to_half((projected[:, :D] + vec_real[4]) * HEAD ** (-0.5))
    keys_b = to_half(projected[:, D:2 * D])
    values_b = to_half(projected[:, 2 * D:] + vec_real[5])
    scores = jnp.einsum('ishd,ithd->ihst', heads_view(queries), heads_view(keys_b))
    log_total = jnp.log(lax.optimization_barrier(jnp.sum(jnp.exp(scores), axis=-1)))
    prob_half = to_half(jnp.exp(scores - log_total[..., None]))
    head_mix = to_half(jnp.einsum('ihst,ithd->ishd', prob_half.astype(jnp.float32), heads_view(values_b)).reshape(-1, D))
    hidden_res = row_block + jnp.dot(head_mix, out_half, preferred_element_type=jnp.float32) + vec_real[6]
    normed_two, inv_two = normalize(hidden_res)
    moe_in = to_half(normed_two * vec_real[2] + vec_real[3])
    exp_logit = jnp.exp(jnp.dot(moe_in, router_half.T, preferred_element_type=jnp.float32))
    route_prob = exp_logit / lax.optimization_barrier(jnp.sum(exp_logit, axis=-1, keepdims=True))
    return (attn_in, normed_one, inv_one, queries, keys_b, values_b, log_total, head_mix, hidden_res, normed_two, inv_two, moe_in, route_prob)

def backward_rows(saved, grad_moe, cot_rows, grad_gate, ids_here, qkv_half, out_half, vec_real, router_half):
    attn_in, normed_one, inv_one, queries, keys_b, values_b, log_total, head_mix, hidden_res, normed_two, inv_two, moe_in, route_prob = saved
    onehot = expert_table(ids_here)
    grad_prob = lax.optimization_barrier(jnp.sum(grad_gate[..., None] * onehot, axis=1))
    grad_logit = route_prob * (grad_prob - lax.optimization_barrier(jnp.sum(route_prob * grad_prob, axis=-1, keepdims=True)))
    logit_half = to_half(grad_logit)
    router_grad = jnp.dot(logit_half.T, moe_in, preferred_element_type=jnp.float32)
    grad_moe = grad_moe + jnp.dot(logit_half, router_half, preferred_element_type=jnp.float32)
    gain_two = lax.optimization_barrier(jnp.sum(grad_moe * normed_two, axis=0))
    shift_two = lax.optimization_barrier(jnp.sum(grad_moe, axis=0))
    grad_res = cot_rows + normalize_back(grad_moe * vec_real[2], normed_two, inv_two)
    res_half = to_half(grad_res)
    bias_out = lax.optimization_barrier(jnp.sum(grad_res, axis=0))
    out_part = jnp.dot(head_mix.T, res_half, preferred_element_type=jnp.float32)
    grad_mix = to_half(jnp.dot(res_half, out_half.T, preferred_element_type=jnp.float32))
    scores = jnp.einsum('ishd,ithd->ihst', heads_view(queries), heads_view(keys_b))
    prob_full = jnp.exp(scores - log_total[..., None])
    prob_half = to_half(prob_full)
    grad_probs = jnp.einsum('ishd,ithd->ihst', heads_view(grad_mix), heads_view(values_b))
    grad_values = jnp.einsum('ihst,ishd->ithd', prob_half.astype(jnp.float32), heads_view(grad_mix))
    grad_scores = prob_full * (grad_probs - lax.optimization_barrier(jnp.sum(prob_full * grad_probs, axis=-1, keepdims=True)))
    score_half = to_half(grad_scores).astype(jnp.float32)
    grad_queries = jnp.einsum('ihst,ithd->ishd', score_half, heads_view(keys_b)) * HEAD ** (-0.5)
    grad_keys = jnp.einsum('ihst,ishd->ithd', score_half, heads_view(queries))
    grad_queries = grad_queries.reshape(-1, D)
    grad_values = grad_values.reshape(-1, D)
    proj_half = to_half(jnp.concatenate([grad_queries, grad_keys.reshape(-1, D), grad_values], axis=1))
    qkv_part = jnp.dot(attn_in.T, proj_half, preferred_element_type=jnp.float32)
    grad_attn = jnp.dot(proj_half, qkv_half.T, preferred_element_type=jnp.float32)
    gain_one = lax.optimization_barrier(jnp.sum(grad_attn * normed_one, axis=0))
    shift_one = lax.optimization_barrier(jnp.sum(grad_attn, axis=0))
    grad_rows = grad_res + normalize_back(grad_attn * vec_real[0], normed_one, inv_one)
    small_part = jnp.stack([gain_one, shift_one, gain_two, shift_two, lax.optimization_barrier(jnp.sum(grad_queries, axis=0)), lax.optimization_barrier(jnp.sum(grad_values, axis=0)), bias_out])
    return (grad_rows, qkv_part, out_part, small_part, router_grad)

def adamw_step(weight, grad, first_m, second_m):
    new_first = BETA_ONE * first_m + (1.0 - BETA_ONE) * grad
    new_second = BETA_TWO * second_m + (1.0 - BETA_TWO) * grad * grad
    step_dir = new_first / CORR_ONE / (jnp.sqrt(new_second / CORR_TWO) + ADAM_EPS)
    return (weight - LEARN_RATE * (step_dir + WEIGHT_DECAY * weight), new_first, new_second)

def reference(tokens, cotangent, expert_ids, slot_pos, qkv_w, qkv_m, qkv_v, out_w, out_m, out_v, vectors, vec_m, vec_v, w_in, w_in_m, w_in_v, w_out, w_out_m, w_out_v, b_in, b_in_m, b_in_v):
    qkv_half = to_half(qkv_w)
    out_half = to_half(out_w)
    vec_half = to_half(vectors)
    vec_real = lax.optimization_barrier(vec_half).astype(jnp.float32)
    router_half = vec_half[7:7 + EXPERTS]
    out_bias = vec_real[7 + EXPERTS:]
    blocks = TOKENS // TOK_DEV
    in_half = to_half(w_in).reshape(D, EXPERTS, FF).transpose(1, 0, 2)
    out_exp = to_half(w_out).reshape(EXPERTS, FF, D)
    bias_in = lax.optimization_barrier(to_half(b_in)).astype(jnp.float32).reshape(EXPERTS, FF)
    tok_blocks = tokens.reshape(blocks, TOK_DEV, D)
    cot_blocks = cotangent.reshape(blocks, TOK_DEV, D)
    id_blocks = expert_ids.reshape(blocks, TOK_DEV, 2)
    slot_blocks = slot_pos.reshape(blocks, TOK_DEV, 2)

    def forward(row_block):
        return forward_rows(row_block, qkv_half, out_half, vec_real, router_half)

    def first_pass(running, inputs):
        row_block, ids_here, slots_here = inputs
        saved = forward(row_block)
        slot_hits, kept_mask = slot_table(ids_here, slots_here)
        packed = jnp.einsum('ts,td->sd', lax.optimization_barrier(jnp.sum(slot_hits, axis=1)), saved[11].astype(jnp.float32), precision=EXACT)
        return (running, to_half(packed))
    unused, dispatched = lax.scan(first_pass, jnp.zeros((), jnp.float32), (tok_blocks, id_blocks, slot_blocks))
    by_expert = dispatched.reshape(blocks, EXPERTS, CAP, D).transpose(1, 0, 2, 3).reshape(EXPERTS, blocks * CAP, D)

    def expert_forward(inputs):
        rows_e, weight_in, weight_out, bias_e = inputs
        pre_act = jnp.dot(rows_e, weight_in, preferred_element_type=jnp.float32) + bias_e
        return jnp.dot(to_half(jax.nn.gelu(pre_act)), weight_out, preferred_element_type=jnp.float32)
    expert_out = lax.map(expert_forward, (by_expert, in_half, out_exp, bias_in))
    out_blocks = expert_out.reshape(EXPERTS, blocks, CAP, D).transpose(1, 0, 2, 3).reshape(blocks, EXPERTS * CAP, D)

    def third_pass(running, inputs):
        row_block, cot_rows, ids_here, slots_here, results = inputs
        saved = forward(row_block)
        chosen, kept_mask = select_rows(results, ids_here, slots_here)
        onehot = expert_table(ids_here)
        chosen = chosen + jnp.einsum('tke,ed->tkd', onehot, out_bias, precision=EXACT)
        gate_vals = jnp.where(kept_mask, jnp.take_along_axis(saved[12], ids_here, axis=1), 0.0)
        mixed_out = saved[8] + lax.optimization_barrier(jnp.sum(gate_vals[..., None] * chosen, axis=1))
        grad_gate = jnp.where(kept_mask, lax.optimization_barrier(jnp.sum(cot_rows[:, None, :] * chosen, axis=-1)), 0.0)
        weighted = gate_vals[..., None] * cot_rows[:, None, :]
        slot_hits, kept_again = slot_table(ids_here, slots_here)
        grad_packed = to_half(jnp.einsum('tks,tkd->sd', slot_hits, weighted, precision=EXACT))
        running = running + jnp.einsum('tke,tkd->ed', onehot, weighted, precision=EXACT)
        return (running, (mixed_out, grad_gate, grad_packed))
    bias_grad, (block_out, grad_gates, grad_packed) = lax.scan(third_pass, jnp.zeros((EXPERTS, D), jnp.float32), (tok_blocks, cot_blocks, id_blocks, slot_blocks, out_blocks))
    grad_expert = grad_packed.reshape(blocks, EXPERTS, CAP, D).transpose(1, 0, 2, 3).reshape(EXPERTS, blocks * CAP, D)

    def expert_backward(inputs):
        rows_e, grads_e, weight_in, weight_out, bias_e = inputs
        pre_act = jnp.dot(rows_e, weight_in, preferred_element_type=jnp.float32) + bias_e
        activated, gelu_back = jax.vjp(jax.nn.gelu, pre_act)
        act_half = to_half(activated)
        grad_act = jnp.dot(grads_e, weight_out.T, preferred_element_type=jnp.float32)
        grad_wout = jnp.dot(act_half.T, grads_e, preferred_element_type=jnp.float32)
        grad_pre = gelu_back(grad_act)[0]
        pre_half = to_half(grad_pre)
        return (jnp.dot(rows_e.T, pre_half, preferred_element_type=jnp.float32), grad_wout, lax.optimization_barrier(jnp.sum(grad_pre, axis=0)), jnp.dot(pre_half, weight_in.T, preferred_element_type=jnp.float32))
    grad_in, grad_out, grad_bias, grad_slots = lax.map(expert_backward, (by_expert, grad_expert, in_half, out_exp, bias_in))
    slot_blocks_grad = grad_slots.reshape(EXPERTS, blocks, CAP, D).transpose(1, 0, 2, 3).reshape(blocks, EXPERTS * CAP, D)

    def last_pass(running, inputs):
        row_block, cot_rows, ids_here, slots_here, slot_grads, grad_gate = inputs
        saved = forward(row_block)
        picked, kept_mask = select_rows(slot_grads, ids_here, slots_here)
        grad_moe = lax.optimization_barrier(jnp.sum(jnp.where(kept_mask[..., None], picked, 0.0), axis=1))
        grad_rows, qkv_part, out_part, small_part, router_part = backward_rows(saved, grad_moe, cot_rows, grad_gate, ids_here, qkv_half, out_half, vec_real, router_half)
        running = (running[0] + qkv_part, running[1] + out_part, running[2] + small_part, running[3] + router_part)
        return (running, grad_rows)
    start = (jnp.zeros((D, 3 * D), jnp.float32), jnp.zeros((D, D), jnp.float32), jnp.zeros((7, D), jnp.float32), jnp.zeros((EXPERTS, D), jnp.float32))
    totals, input_grad = lax.scan(last_pass, start, (tok_blocks, cot_blocks, id_blocks, slot_blocks, slot_blocks_grad, grad_gates))
    qkv_grad, out_grad = (totals[0], totals[1])
    vec_grad = jnp.concatenate([totals[2], totals[3], bias_grad], axis=0)
    branch_bias_grad = jnp.concatenate([vec_grad[6:7], vec_grad[7 + EXPERTS:]], axis=0)
    w_in_grad = grad_in.transpose(1, 0, 2).reshape(D, EXPERTS * FF)
    w_out_grad = grad_out.reshape(EXPERTS * FF, D)
    b_in_grad = grad_bias.reshape(EXPERTS * FF)
    qkv_new, qkv_m_new, qkv_v_new = adamw_step(qkv_w, qkv_grad, qkv_m, qkv_v)
    out_new, out_m_new, out_v_new = adamw_step(out_w, out_grad, out_m, out_v)
    vec_new, vec_m_new, vec_v_new = adamw_step(vectors, vec_grad, vec_m, vec_v)
    w_in_new, w_in_m_new, w_in_v_new = adamw_step(w_in, w_in_grad, w_in_m, w_in_v)
    w_out_new, w_out_m_new, w_out_v_new = adamw_step(w_out, w_out_grad, w_out_m, w_out_v)
    b_in_new, b_in_m_new, b_in_v_new = adamw_step(b_in, b_in_grad, b_in_m, b_in_v)
    return (block_out.reshape(TOKENS, D), input_grad.reshape(TOKENS, D), qkv_grad, qkv_new, qkv_m_new, qkv_v_new, out_grad, out_new, out_m_new, out_v_new, vec_grad, vec_new, vec_m_new, vec_v_new, w_in_grad, w_in_new, w_in_m_new, w_in_v_new, w_out_grad, w_out_new, w_out_m_new, w_out_v_new, b_in_grad, b_in_new, b_in_m_new, b_in_v_new, branch_bias_grad)
```

```python
import jax
import jax.numpy as jnp
from jax import lax
from jax.sharding import Mesh, PartitionSpec as P

D = 768
HEADS = 12
HEAD = 64
FF = 3072
EXPERTS = 16
SEQ = 197
CAP = 25


LEARN_RATE = 0.15
BETA_ONE = 0.9
BETA_TWO = 0.999
ADAM_EPS = 1e-08
WEIGHT_DECAY = 0.1
CORR_ONE = 1.0 - BETA_ONE**2
CORR_TWO = 1.0 - BETA_TWO**2
NORM_EPS = 1e-06
EXACT = lax.Precision.HIGHEST


def to_half(values):
    return values.astype(jnp.bfloat16)


def heads_split(values):
    return values.reshape(-1, SEQ, HEADS, HEAD)


def normalize(values):
    average = jnp.mean(values, axis=-1, keepdims=True)
    centered = values - average
    inv_std = lax.rsqrt(jnp.mean(centered * centered, axis=-1, keepdims=True) + NORM_EPS)
    return (centered * inv_std, inv_std)


def normalize_back(grad_norm, normed, inv_std):
    return inv_std * (
        grad_norm
        - jnp.mean(grad_norm, axis=-1, keepdims=True)
        - normed * jnp.mean(grad_norm * normed, axis=-1, keepdims=True)
    )


def expert_table(ids_here):
    return (ids_here[..., None] == jnp.arange(EXPERTS)[None, None, :]).astype(jnp.float32)


def slot_table(ids_here, slots_here):
    kept_mask = slots_here >= 0
    target = ids_here * CAP + slots_here
    slot_hits = (target[..., None] == jnp.arange(EXPERTS * CAP)[None, None, :]) & kept_mask[
        ..., None
    ]
    return (slot_hits.astype(jnp.float32), kept_mask)


def select_rows(results, ids_here, slots_here):
    kept_mask = slots_here >= 0
    flat_index = jnp.where(kept_mask, ids_here * CAP + slots_here, 0)
    return (jnp.take(results, flat_index, axis=0), kept_mask)


def forward_rows(row_block, qkv_half, out_half, vec_real, router_half):
    normed_one, inv_one = normalize(row_block)
    attn_in = to_half(normed_one * vec_real[0] + vec_real[1])
    projected = jnp.dot(attn_in, qkv_half, preferred_element_type=jnp.float32)
    queries = to_half((projected[:, :D] + vec_real[4]) * HEAD ** (-0.5))
    keys_b = to_half(projected[:, D : 2 * D])
    values_b = to_half(projected[:, 2 * D :] + vec_real[5])
    scores = jnp.einsum(
        "ishd,ithd->ihst",
        heads_split(queries),
        heads_split(keys_b),
        preferred_element_type=jnp.float32,
    )
    log_total = jnp.log(jnp.sum(jnp.exp(scores), axis=-1))
    prob_half = to_half(jnp.exp(scores - log_total[..., None]))
    head_mix = to_half(
        jnp.einsum(
            "ihst,ithd->ishd", prob_half, heads_split(values_b), preferred_element_type=jnp.float32
        ).reshape(-1, D)
    )
    hidden_res = (
        row_block + jnp.dot(head_mix, out_half, preferred_element_type=jnp.float32) + vec_real[6]
    )
    normed_two, inv_two = normalize(hidden_res)
    moe_in = to_half(normed_two * vec_real[2] + vec_real[3])
    exp_logit = jnp.exp(
        jnp.einsum("td,ed->te", moe_in, router_half, preferred_element_type=jnp.float32)
    )
    route_prob = exp_logit / jnp.sum(exp_logit, axis=-1, keepdims=True)
    return (
        attn_in,
        normed_one,
        inv_one,
        queries,
        keys_b,
        values_b,
        log_total,
        head_mix,
        hidden_res,
        normed_two,
        inv_two,
        moe_in,
        route_prob,
    )


def backward_rows(
    saved, grad_moe, cot_rows, grad_gate, ids_here, qkv_half, out_half, vec_real, router_half
):
    (
        attn_in,
        normed_one,
        inv_one,
        queries,
        keys_b,
        values_b,
        log_total,
        head_mix,
        hidden_res,
        normed_two,
        inv_two,
        moe_in,
        route_prob,
    ) = saved
    onehot = expert_table(ids_here)
    grad_prob = jnp.sum(grad_gate[..., None] * onehot, axis=1)
    grad_logit = route_prob * (grad_prob - jnp.sum(route_prob * grad_prob, axis=-1, keepdims=True))
    logit_half = to_half(grad_logit)
    router_grad = jnp.einsum("te,td->ed", logit_half, moe_in, preferred_element_type=jnp.float32)
    grad_moe = grad_moe + jnp.dot(logit_half, router_half, preferred_element_type=jnp.float32)
    gain_two = jnp.sum(grad_moe * normed_two, axis=0)
    shift_two = jnp.sum(grad_moe, axis=0)
    grad_res = cot_rows + normalize_back(grad_moe * vec_real[2], normed_two, inv_two)
    res_half = to_half(grad_res)
    bias_out = jnp.sum(grad_res, axis=0)
    out_part = jnp.einsum("tf,td->fd", head_mix, res_half, preferred_element_type=jnp.float32)
    grad_mix = to_half(
        jnp.einsum("td,fd->tf", res_half, out_half, preferred_element_type=jnp.float32)
    )
    scores = jnp.einsum(
        "ishd,ithd->ihst",
        heads_split(queries),
        heads_split(keys_b),
        preferred_element_type=jnp.float32,
    )
    prob_full = jnp.exp(scores - log_total[..., None])
    prob_half = to_half(prob_full)
    grad_probs = jnp.einsum(
        "ishd,ithd->ihst",
        heads_split(grad_mix),
        heads_split(values_b),
        preferred_element_type=jnp.float32,
    )
    grad_values = jnp.einsum(
        "ihst,ishd->ithd", prob_half, heads_split(grad_mix), preferred_element_type=jnp.float32
    )
    grad_scores = prob_full * (grad_probs - jnp.sum(prob_full * grad_probs, axis=-1, keepdims=True))
    score_half = to_half(grad_scores)
    grad_queries = jnp.einsum(
        "ihst,ithd->ishd", score_half, heads_split(keys_b), preferred_element_type=jnp.float32
    ) * HEAD ** (-0.5)
    grad_keys = jnp.einsum(
        "ihst,ishd->ithd", score_half, heads_split(queries), preferred_element_type=jnp.float32
    )
    grad_queries = grad_queries.reshape(-1, D)
    grad_values = grad_values.reshape(-1, D)
    proj_half = to_half(
        jnp.concatenate([grad_queries, grad_keys.reshape(-1, D), grad_values], axis=1)
    )
    qkv_part = jnp.einsum("td,tq->dq", attn_in, proj_half, preferred_element_type=jnp.float32)
    grad_attn = jnp.einsum("tq,dq->td", proj_half, qkv_half, preferred_element_type=jnp.float32)
    gain_one = jnp.sum(grad_attn * normed_one, axis=0)
    shift_one = jnp.sum(grad_attn, axis=0)
    grad_rows = grad_res + normalize_back(grad_attn * vec_real[0], normed_one, inv_one)
    small_part = jnp.stack(
        [
            gain_one,
            shift_one,
            gain_two,
            shift_two,
            jnp.sum(grad_queries, axis=0),
            jnp.sum(grad_values, axis=0),
            bias_out,
        ]
    )
    return (grad_rows, qkv_part, out_part, small_part, router_grad)


def adamw_step(weight, grad, first_m, second_m):
    new_first = BETA_ONE * first_m + (1.0 - BETA_ONE) * grad
    new_second = BETA_TWO * second_m + (1.0 - BETA_TWO) * grad * grad
    step_dir = new_first / CORR_ONE / (jnp.sqrt(new_second / CORR_TWO) + ADAM_EPS)
    return (weight - LEARN_RATE * (step_dir + WEIGHT_DECAY * weight), new_first, new_second)


def body_any(
    tokens,
    cotangent,
    expert_ids,
    slot_pos,
    qkv_w,
    qkv_m,
    qkv_v,
    out_w,
    out_m,
    out_v,
    vectors,
    vec_m,
    vec_v,
    w_in,
    w_in_m,
    w_in_v,
    w_out,
    w_out_m,
    w_out_v,
    b_in,
    b_in_m,
    b_in_v,
):
    qkv_shard = to_half(qkv_w)
    out_shard = to_half(out_w)
    vec_shard = to_half(vectors)
    qkv_half, out_half, vec_half = (
        lax.all_gather(qkv_shard, ("dp", "group"), axis=0, tiled=True),
        lax.all_gather(out_shard, ("dp", "group"), axis=0, tiled=True),
        lax.all_gather(vec_shard, ("dp", "group"), axis=1, tiled=True),
    )
    win_full, wout_full, bin_full = (
        lax.all_gather(to_half(w_in), "group", axis=0, tiled=True),
        lax.all_gather(to_half(w_out), "group", axis=1, tiled=True),
        lax.all_gather(to_half(b_in), "group", axis=0, tiled=True),
    )
    vec_real = vec_half.astype(jnp.float32)
    router_half = vec_half[7 : 7 + EXPERTS]
    out_bias = vec_real[7 + EXPERTS :]
    hid_cols = win_full.shape[1]
    local_exp = max(1, hid_cols // FF)
    hid_width = hid_cols // local_exp
    split_count = FF // hid_width
    dp_count = lax.axis_size("dp")
    weight_in = win_full.reshape(D, local_exp, hid_width).transpose(1, 0, 2)
    weight_out = wout_full.reshape(local_exp, hid_width, D)
    bias_in = bin_full.astype(jnp.float32).reshape(local_exp, hid_width)

    def spread(buffer):
        return jnp.repeat(buffer.reshape(EXPERTS, CAP, D), split_count, axis=0)

    def to_experts(arrived):
        return (
            arrived.reshape(dp_count, local_exp, CAP, D)
            .transpose(1, 0, 2, 3)
            .reshape(local_exp, dp_count * CAP, D)
        )

    def to_sources(expert_rows):
        return (
            expert_rows.reshape(local_exp, dp_count, CAP, D)
            .transpose(1, 0, 2, 3)
            .reshape(dp_count * local_exp, CAP, D)
        )

    def join_parts(arrived):
        return jnp.sum(arrived.reshape(EXPERTS, split_count, CAP, D), axis=1).reshape(
            EXPERTS * CAP, D
        )

    saved = forward_rows(tokens, qkv_half, out_half, vec_real, router_half)
    slot_hits, kept_mask = slot_table(expert_ids, slot_pos)
    packed = to_half(
        jnp.einsum(
            "ts,td->sd",
            to_half(jnp.sum(slot_hits, axis=1)),
            saved[11],
            preferred_element_type=jnp.float32,
        )
    )
    routed_rows = to_experts(
        lax.all_to_all(spread(packed), "dp", split_axis=0, concat_axis=0, tiled=True)
    )
    pre_act = (
        jnp.einsum("erd,edh->erh", routed_rows, weight_in, preferred_element_type=jnp.float32)
        + bias_in[:, None, :]
    )
    expert_res = jnp.einsum(
        "erh,ehd->erd",
        to_half(jax.nn.gelu(pre_act)),
        weight_out,
        preferred_element_type=jnp.float32,
    )
    combined = join_parts(
        lax.all_to_all(
            to_sources(expert_res).astype(jnp.bfloat16),
            "dp",
            split_axis=0,
            concat_axis=0,
            tiled=True,
        ).astype(jnp.float32)
    )
    chosen, kept_mask = select_rows(combined, expert_ids, slot_pos)
    onehot = expert_table(expert_ids)
    chosen = chosen + jnp.einsum("tke,ed->tkd", onehot, out_bias, precision=EXACT)
    gate_vals = jnp.where(kept_mask, jnp.take_along_axis(saved[12], expert_ids, axis=1), 0.0)
    block_out = saved[8] + jnp.sum(gate_vals[..., None] * chosen, axis=1)
    grad_gate = jnp.where(kept_mask, jnp.sum(cotangent[:, None, :] * chosen, axis=-1), 0.0)
    weighted = gate_vals[..., None] * cotangent[:, None, :]
    grad_packed = to_half(jnp.einsum("tks,tkd->sd", slot_hits, weighted, precision=EXACT))
    bias_grad = jnp.einsum("tke,tkd->ed", onehot, weighted, precision=EXACT)
    grad_routed = to_experts(
        lax.all_to_all(spread(grad_packed), "dp", split_axis=0, concat_axis=0, tiled=True)
    )
    activated, gelu_back = jax.vjp(jax.nn.gelu, pre_act)
    act_half = to_half(activated)
    grad_act = jnp.einsum(
        "erd,ehd->erh", grad_routed, weight_out, preferred_element_type=jnp.float32
    )
    grad_wout = jnp.einsum(
        "erh,erd->ehd", act_half, grad_routed, preferred_element_type=jnp.float32
    )
    grad_pre = gelu_back(grad_act)[0]
    grad_bias_in = jnp.sum(grad_pre, axis=1)
    pre_half = to_half(grad_pre)
    grad_win = jnp.einsum("erd,erh->edh", routed_rows, pre_half, preferred_element_type=jnp.float32)
    grad_inputs = jnp.einsum(
        "erh,edh->erd", pre_half, weight_in, preferred_element_type=jnp.float32
    )
    slot_grads = join_parts(
        lax.all_to_all(
            to_sources(grad_inputs).astype(jnp.bfloat16),
            "dp",
            split_axis=0,
            concat_axis=0,
            tiled=True,
        ).astype(jnp.float32)
    )
    w_in_grad, w_out_grad, b_in_grad = (
        lax.psum_scatter(
            grad_win.transpose(1, 0, 2).reshape(D, hid_cols).astype(jnp.bfloat16),
            "group",
            scatter_dimension=0,
            tiled=True,
        ).astype(jnp.float32),
        lax.psum_scatter(
            grad_wout.reshape(hid_cols, D).astype(jnp.bfloat16),
            "group",
            scatter_dimension=1,
            tiled=True,
        ).astype(jnp.float32),
        lax.psum_scatter(
            grad_bias_in.reshape(hid_cols).astype(jnp.bfloat16),
            "group",
            scatter_dimension=0,
            tiled=True,
        ).astype(jnp.float32),
    )
    picked, kept_mask = select_rows(slot_grads, expert_ids, slot_pos)
    grad_moe = jnp.sum(jnp.where(kept_mask[..., None], picked, 0.0), axis=1)
    input_grad, qkv_part, out_part, small_part, router_grad = backward_rows(
        saved, grad_moe, cotangent, grad_gate, expert_ids, qkv_half, out_half, vec_real, router_half
    )
    vec_part = jnp.concatenate([small_part, router_grad, bias_grad], axis=0)
    qkv_grad, out_grad, vec_grad = (
        lax.psum_scatter(qkv_part, ("dp", "group"), scatter_dimension=0, tiled=True),
        lax.psum_scatter(out_part, ("dp", "group"), scatter_dimension=0, tiled=True),
        lax.psum_scatter(vec_part, ("dp", "group"), scatter_dimension=1, tiled=True),
    )
    branch_bias_grad = jnp.concatenate([vec_grad[6:7], vec_grad[7 + EXPERTS :]], axis=0)
    qkv_new, qkv_m_new, qkv_v_new = adamw_step(qkv_w, qkv_grad, qkv_m, qkv_v)
    out_new, out_m_new, out_v_new = adamw_step(out_w, out_grad, out_m, out_v)
    vec_new, vec_m_new, vec_v_new = adamw_step(vectors, vec_grad, vec_m, vec_v)
    w_in_new, w_in_m_new, w_in_v_new = adamw_step(w_in, w_in_grad, w_in_m, w_in_v)
    w_out_new, w_out_m_new, w_out_v_new = adamw_step(w_out, w_out_grad, w_out_m, w_out_v)
    b_in_new, b_in_m_new, b_in_v_new = adamw_step(b_in, b_in_grad, b_in_m, b_in_v)
    return (
        block_out,
        input_grad,
        qkv_grad,
        qkv_new,
        qkv_m_new,
        qkv_v_new,
        out_grad,
        out_new,
        out_m_new,
        out_v_new,
        vec_grad,
        vec_new,
        vec_m_new,
        vec_v_new,
        w_in_grad,
        w_in_new,
        w_in_m_new,
        w_in_v_new,
        w_out_grad,
        w_out_new,
        w_out_m_new,
        w_out_v_new,
        b_in_grad,
        b_in_new,
        b_in_m_new,
        b_in_v_new,
        branch_bias_grad,
    )


AXES = ("y", "x", "core", "group")
CHIPS = ("y", "x", "group")
COLUMN = ("core", "group")
SWAP = [(0, 1), (1, 0)]
WIDE = 3200
SHARD = 24


def exact_dot(left, right, dims):
    return lax.dot_general(left, right, (dims, ((), ())), preferred_element_type=jnp.float32)


def shift_perm(step):
    return [(i, (i + step) % 4) for i in range(4)]


def place():
    return tuple(lax.axis_index(name) for name in AXES)


def join_swap(rows, axis_name):
    return jnp.concatenate([rows, lax.ppermute(rows, axis_name, SWAP)], axis=0)


def gather_line(shard):
    return [shard] + [lax.ppermute(shard, "group", shift_perm(step)) for step in (1, 2, 3)]


def gather_plane(blocks):
    first = jnp.concatenate(blocks[:2], axis=0)
    second = jnp.concatenate(blocks[2:], axis=0)
    first, second = join_swap(first, "x"), join_swap(second, "y")
    first, second = join_swap(first, "y"), join_swap(second, "x")
    return jnp.concatenate([join_swap(first, "core"), join_swap(second, "core")], axis=0)


def fold_swap(rows, axis_name):
    half = rows.shape[0] // 2
    arrived = lax.ppermute(rows[half:], axis_name, SWAP)
    return to_half(rows[:half].astype(jnp.float32) + arrived.astype(jnp.float32))


def scatter_sum(rows):
    half = rows.shape[0] // 2
    first, second = fold_swap(rows[:half], "core"), fold_swap(rows[half:], "core")
    first, second = fold_swap(first, "y"), fold_swap(second, "x")
    first, second = fold_swap(first, "x"), fold_swap(second, "y")
    blocks = [first[:SHARD], first[SHARD:], second[:SHARD], second[SHARD:]]
    total = blocks[0].astype(jnp.float32)
    for step in (1, 2, 3):
        total = total + lax.ppermute(blocks[step], "group", shift_perm(-step)).astype(jnp.float32)
    return total


def row_order():
    row_y, row_x, core, line = place()
    spot = jnp.arange(D)
    half = spot // 384
    other = (spot // 192) % 2
    outer = (spot // 96) % 2
    inner = (spot // 48) % 2
    step = half * 2 + (spot // SHARD) % 2
    y_rel = jnp.where(half == 0, outer, inner)
    x_rel = jnp.where(half == 0, inner, outer)
    owner = (((row_y ^ y_rel) * 2 + (row_x ^ x_rel)) * 2 + (core ^ other)) * 4 + (line - step) % 4
    feature = owner * SHARD + spot % SHARD
    return to_half(feature[:, None] == jnp.arange(D)[None, :])


def column_pairs(turn):
    pairs = []
    for core in range(2):
        for line in range(4):
            part = (line + turn) % 4
            pairs.append((core * 4 + line, (part % 2) * 4 + 2 * core + part // 2))
    return pairs


def to_hosts(rows):
    row_y, row_x, core, line = place()
    parts = rows.reshape(rows.shape[0], 4, -1)
    arrived = []
    for turn in range(4):
        part = lax.dynamic_index_in_dim(parts, (line + turn) % 4, axis=1, keepdims=False)
        arrived.append(lax.ppermute(to_half(part), COLUMN, column_pairs(turn)))
    return arrived


def settle(arrived):
    row_y, row_x, core, line = place()
    stacked = jnp.stack(arrived, axis=0)
    here = 2 * (line % 2) + core
    pieces = [
        lax.dynamic_index_in_dim(stacked, (here - piece) % 4, axis=0, keepdims=False)
        for piece in range(4)
    ]
    return jnp.concatenate(pieces, axis=0)


def to_owners(grads):
    row_y, row_x, core, line = place()
    here = 2 * (line % 2) + core
    pieces = to_half(grads).reshape(4, -1, grads.shape[1])
    arrived = []
    for turn in range(4):
        piece = lax.dynamic_index_in_dim(pieces, (here - turn) % 4, axis=0, keepdims=False)
        back = [(host, owner) for owner, host in column_pairs(turn)]
        arrived.append(lax.ppermute(piece, COLUMN, back))
    stacked = jnp.stack(arrived, axis=0)
    parts = [
        lax.dynamic_index_in_dim(stacked, (part - line) % 4, axis=0, keepdims=False)
        for part in range(4)
    ]
    return jnp.concatenate(parts, axis=1).astype(jnp.float32)


BIAS_PAIRS = [(i, (i % 2) * 4 + i // 2) for i in range(8)]


def body_column(
    tokens,
    cotangent,
    expert_ids,
    slot_pos,
    qkv_w,
    qkv_m,
    qkv_v,
    out_w,
    out_m,
    out_v,
    vectors,
    vec_m,
    vec_v,
    w_in,
    w_in_m,
    w_in_v,
    w_out,
    w_out_m,
    w_out_v,
    b_in,
    b_in_m,
    b_in_v,
):
    f32 = jnp.float32
    shard = jnp.concatenate(
        [
            to_half(qkv_w),
            to_half(out_w),
            jnp.pad(to_half(vectors.T), ((0, 0), (0, WIDE - 4 * D - vectors.shape[0]))),
        ],
        axis=1,
    )
    blocks = gather_line(shard)
    blocks, w_in_now, w_out_now, b_in_now = lax.optimization_barrier(
        (blocks, w_in, w_out, b_in)
    )
    gathered = gather_plane(blocks)
    win_parts = to_hosts(w_in_now)
    wout_parts = to_hosts(w_out_now.T)
    bias_in = lax.ppermute(to_half(b_in_now), COLUMN, BIAS_PAIRS).astype(f32)

    order = row_order()
    qkv_half = gathered[:, : 3 * D]
    out_half = gathered[:, 3 * D : 4 * D]
    vec_real = exact_dot(gathered[:, 4 * D :], order, ((0,), (0,)))[:39]
    router_half = to_half(vec_real[7 : 7 + EXPERTS])
    out_bias = to_half(vec_real[7 + EXPERTS :])

    normed_one, inv_one = normalize(tokens)
    attn_in = to_half(normed_one * vec_real[0] + vec_real[1])
    attn_rel = to_half(exact_dot(attn_in, order, ((1,), (1,))))
    projected = jnp.dot(attn_rel, qkv_half, preferred_element_type=f32)
    queries = to_half((projected[:, :D] + vec_real[4]) * HEAD ** (-0.5))
    keys_b = to_half(projected[:, D : 2 * D])
    values_b = to_half(projected[:, 2 * D :] + vec_real[5])
    scores = jnp.einsum(
        "ishd,ithd->ihst", heads_split(queries), heads_split(keys_b), preferred_element_type=f32
    )
    log_total = jnp.log(jnp.sum(jnp.exp(scores), axis=-1))
    prob_half = to_half(jnp.exp(scores - log_total[..., None]))
    head_mix = to_half(
        jnp.einsum(
            "ihst,ithd->ishd", prob_half, heads_split(values_b), preferred_element_type=f32
        ).reshape(-1, D)
    )
    mix_rel = to_half(exact_dot(head_mix, order, ((1,), (1,))))
    hidden_res = tokens + jnp.dot(mix_rel, out_half, preferred_element_type=f32) + vec_real[6]
    normed_two, inv_two = normalize(hidden_res)
    moe_in = to_half(normed_two * vec_real[2] + vec_real[3])
    exp_logit = jnp.exp(exact_dot(moe_in, router_half, ((1,), (1,))))
    route_prob = exp_logit / jnp.sum(exp_logit, axis=-1, keepdims=True)

    kept_mask = slot_pos >= 0
    onehot = expert_table(expert_ids)
    slot_hits = to_half(slot_table(expert_ids, slot_pos)[0])
    hits_both = slot_hits[:, 0] + slot_hits[:, 1]
    gate_vals = jnp.where(kept_mask, jnp.sum(onehot * route_prob[:, None, :], axis=-1), 0.0)
    packed = to_half(exact_dot(hits_both, moe_in, ((0,), (0,))))
    weighted = to_half(gate_vals[..., None] * cotangent[:, None, :])
    grad_packed = to_half(
        exact_dot(slot_hits[:, 0], weighted[:, 0], ((0,), (0,)))
        + exact_dot(slot_hits[:, 1], weighted[:, 1], ((0,), (0,)))
    )
    bias_grad = jnp.einsum(
        "te,td->ed", jnp.sum(onehot * gate_vals[..., None], axis=1), cotangent, precision=EXACT
    )

    def both(first, second):
        return jnp.concatenate(
            [first.reshape(EXPERTS, CAP, D), second.reshape(EXPERTS, CAP, D)], axis=1
        )

    def swap_chips(rows):
        return lax.all_to_all(rows, CHIPS, split_axis=0, concat_axis=0, tiled=True)

    routed_own = swap_chips(both(packed, grad_packed))
    routed = jnp.concatenate([routed_own, lax.ppermute(routed_own, "core", SWAP)], axis=0)
    rows_in = routed[:, :CAP].reshape(-1, D)
    grads_in = routed[:, CAP:].reshape(-1, D)

    weight_in = settle(win_parts)
    weight_out = settle(wout_parts)
    pre_act = jnp.dot(rows_in, weight_in, preferred_element_type=f32) + bias_in[None, :]
    activated, gelu_back = jax.vjp(jax.nn.gelu, pre_act)
    act_half = to_half(activated)
    expert_res = exact_dot(act_half, weight_out, ((1,), (1,)))
    grad_act = exact_dot(grads_in, weight_out, ((1,), (0,)))
    grad_wout = exact_dot(grads_in, act_half, ((0,), (0,)))
    grad_pre = gelu_back(grad_act)[0]
    grad_bias_in = jnp.sum(grad_pre, axis=0)
    pre_half = to_half(grad_pre)
    grad_win = exact_dot(rows_in, pre_half, ((0,), (0,)))
    grad_slots = exact_dot(pre_half, weight_in, ((1,), (1,)))

    def halves_sum(rows):
        count = rows.shape[0] // 2
        return to_half(rows[:count] + lax.ppermute(to_half(rows[count:]), "core", SWAP))

    returned = swap_chips(both(halves_sum(expert_res), halves_sum(grad_slots)))
    combined = returned[:, :CAP].reshape(-1, D)
    slot_grads = returned[:, CAP:].reshape(-1, D)
    w_out_grad = to_owners(grad_wout).T
    w_in_grad = to_owners(grad_win)
    b_in_grad = lax.ppermute(grad_bias_in, COLUMN, [(host, owner) for owner, host in BIAS_PAIRS])

    onehot_half = to_half(onehot)
    chosen = jnp.stack(
        [
            exact_dot(slot_hits[:, k], combined, ((1,), (0,)))
            + exact_dot(onehot_half[:, k], out_bias, ((1,), (0,)))
            for k in range(2)
        ],
        axis=1,
    )
    block_out = hidden_res + jnp.sum(gate_vals[..., None] * chosen, axis=1)
    grad_gate = jnp.where(kept_mask, jnp.sum(cotangent[:, None, :] * chosen, axis=-1), 0.0)
    grad_moe = exact_dot(hits_both, slot_grads, ((1,), (0,)))

    grad_prob = jnp.sum(grad_gate[..., None] * onehot, axis=1)
    grad_logit = route_prob * (grad_prob - jnp.sum(route_prob * grad_prob, axis=-1, keepdims=True))
    logit_half = to_half(grad_logit)
    router_grad = exact_dot(logit_half, moe_in, ((0,), (0,)))
    grad_moe = grad_moe + jnp.dot(logit_half, router_half, preferred_element_type=f32)
    gain_two = jnp.sum(grad_moe * normed_two, axis=0)
    shift_two = jnp.sum(grad_moe, axis=0)
    grad_res = cotangent + normalize_back(grad_moe * vec_real[2], normed_two, inv_two)
    res_half = to_half(grad_res)
    bias_out = jnp.sum(grad_res, axis=0)
    out_part = exact_dot(mix_rel, res_half, ((0,), (0,)))
    mix_back = to_half(exact_dot(res_half, out_half, ((1,), (1,))))
    grad_mix = to_half(jnp.dot(mix_back, order, preferred_element_type=f32))
    prob_full = jnp.exp(scores - log_total[..., None])
    prob_half = to_half(prob_full)
    grad_probs = jnp.einsum(
        "ishd,ithd->ihst", heads_split(grad_mix), heads_split(values_b), preferred_element_type=f32
    )
    grad_values = jnp.einsum(
        "ihst,ishd->ithd", prob_half, heads_split(grad_mix), preferred_element_type=f32
    )
    grad_scores = prob_full * (grad_probs - jnp.sum(prob_full * grad_probs, axis=-1, keepdims=True))
    score_half = to_half(grad_scores)
    grad_queries = jnp.einsum(
        "ihst,ithd->ishd", score_half, heads_split(keys_b), preferred_element_type=f32
    ) * HEAD ** (-0.5)
    grad_keys = jnp.einsum(
        "ihst,ishd->ithd", score_half, heads_split(queries), preferred_element_type=f32
    )
    grad_queries = grad_queries.reshape(-1, D)
    grad_values = grad_values.reshape(-1, D)
    proj_half = to_half(
        jnp.concatenate([grad_queries, grad_keys.reshape(-1, D), grad_values], axis=1)
    )
    qkv_part = exact_dot(attn_rel, proj_half, ((0,), (0,)))
    attn_back = exact_dot(proj_half, qkv_half, ((1,), (1,)))
    grad_attn = jnp.dot(attn_back, order.astype(f32), precision=EXACT)
    gain_one = jnp.sum(grad_attn * normed_one, axis=0)
    shift_one = jnp.sum(grad_attn, axis=0)
    input_grad = grad_res + normalize_back(grad_attn * vec_real[0], normed_one, inv_one)
    small_part = jnp.stack(
        [
            gain_one,
            shift_one,
            gain_two,
            shift_two,
            jnp.sum(grad_queries, axis=0),
            jnp.sum(grad_values, axis=0),
            bias_out,
        ]
    )
    vec_part = to_half(jnp.concatenate([small_part, router_grad, bias_grad], axis=0))
    vec_rel = to_half(exact_dot(order, vec_part, ((1,), (1,))))
    summed = scatter_sum(
        jnp.concatenate(
            [
                to_half(qkv_part),
                to_half(out_part),
                jnp.pad(vec_rel, ((0, 0), (0, WIDE - 4 * D - vec_rel.shape[1]))),
            ],
            axis=1,
        )
    )
    qkv_grad = summed[:, : 3 * D]
    out_grad = summed[:, 3 * D : 4 * D]
    vec_grad = summed[:, 4 * D : 4 * D + vectors.shape[0]].T
    branch_bias_grad = jnp.concatenate([vec_grad[6:7], vec_grad[7 + EXPERTS :]], axis=0)
    qkv_new, qkv_m_new, qkv_v_new = adamw_step(qkv_w, qkv_grad, qkv_m, qkv_v)
    out_new, out_m_new, out_v_new = adamw_step(out_w, out_grad, out_m, out_v)
    vec_new, vec_m_new, vec_v_new = adamw_step(vectors, vec_grad, vec_m, vec_v)
    w_in_new, w_in_m_new, w_in_v_new = adamw_step(w_in, w_in_grad, w_in_m, w_in_v)
    w_out_new, w_out_m_new, w_out_v_new = adamw_step(w_out, w_out_grad, w_out_m, w_out_v)
    b_in_new, b_in_m_new, b_in_v_new = adamw_step(b_in, b_in_grad, b_in_m, b_in_v)
    return (
        block_out,
        input_grad,
        qkv_grad,
        qkv_new,
        qkv_m_new,
        qkv_v_new,
        out_grad,
        out_new,
        out_m_new,
        out_v_new,
        vec_grad,
        vec_new,
        vec_m_new,
        vec_v_new,
        w_in_grad,
        w_in_new,
        w_in_m_new,
        w_in_v_new,
        w_out_grad,
        w_out_new,
        w_out_m_new,
        w_out_v_new,
        b_in_grad,
        b_in_new,
        b_in_m_new,
        b_in_v_new,
        branch_bias_grad,
    )


def solution(mesh):
    if mesh.shape["dp"] == 8 and mesh.shape["group"] == 4:
        inner = Mesh(mesh.devices.reshape(2, 2, 2, 4), AXES)
        body, dp, group, both = body_column, ("y", "x", "core"), "group", AXES
    else:
        inner, body, dp, group, both = mesh, body_any, "dp", "group", ("dp", "group")
    return jax.shard_map(
        body,
        mesh=inner,
        in_specs=(
            P(both, None),
            P(both, None),
            P(both, None),
            P(both, None),
            P(both, None),
            P(both, None),
            P(both, None),
            P(both, None),
            P(both, None),
            P(both, None),
            P(None, both),
            P(None, both),
            P(None, both),
            P(group, dp),
            P(group, dp),
            P(group, dp),
            P(dp, group),
            P(dp, group),
            P(dp, group),
            P(both),
            P(both),
            P(both),
        ),
        out_specs=(
            P(both, None),
            P(both, None),
            P(both, None),
            P(both, None),
            P(both, None),
            P(both, None),
            P(both, None),
            P(both, None),
            P(both, None),
            P(both, None),
            P(None, both),
            P(None, both),
            P(None, both),
            P(None, both),
            P(group, dp),
            P(group, dp),
            P(group, dp),
            P(group, dp),
            P(dp, group),
            P(dp, group),
            P(dp, group),
            P(dp, group),
            P(both),
            P(both),
            P(both),
            P(both),
            P(None, both),
        ),
        check_vma=False,
    )
```

```python
import jax
import jax.numpy as jnp
from jax import lax
from jax.experimental import pallas as pl
from jax.experimental.pallas import tpu as pltpu
from jax.sharding import Mesh, PartitionSpec as P

D = 768
HEADS = 12
HEAD = 64
FF = 3072
EXPERTS = 16
SEQ = 197
CAP = 25


LEARN_RATE = 0.15
BETA_ONE = 0.9
BETA_TWO = 0.999
ADAM_EPS = 1e-08
WEIGHT_DECAY = 0.1
CORR_ONE = 1.0 - BETA_ONE**2
CORR_TWO = 1.0 - BETA_TWO**2
NORM_EPS = 1e-06
EXACT = lax.Precision.HIGHEST


def to_half(values):
    return values.astype(jnp.bfloat16)


def heads_split(values):
    return values.reshape(-1, SEQ, HEADS, HEAD)


def normalize(values):
    average = jnp.mean(values, axis=-1, keepdims=True)
    centered = values - average
    inv_std = lax.rsqrt(jnp.mean(centered * centered, axis=-1, keepdims=True) + NORM_EPS)
    return (centered * inv_std, inv_std)


def normalize_back(grad_norm, normed, inv_std):
    return inv_std * (
        grad_norm
        - jnp.mean(grad_norm, axis=-1, keepdims=True)
        - normed * jnp.mean(grad_norm * normed, axis=-1, keepdims=True)
    )


def expert_table(ids_here):
    return (ids_here[..., None] == jnp.arange(EXPERTS)[None, None, :]).astype(jnp.float32)


def slot_table(ids_here, slots_here):
    kept_mask = slots_here >= 0
    target = ids_here * CAP + slots_here
    slot_hits = (target[..., None] == jnp.arange(EXPERTS * CAP)[None, None, :]) & kept_mask[
        ..., None
    ]
    return (slot_hits.astype(jnp.float32), kept_mask)


def select_rows(results, ids_here, slots_here):
    kept_mask = slots_here >= 0
    flat_index = jnp.where(kept_mask, ids_here * CAP + slots_here, 0)
    return (jnp.take(results, flat_index, axis=0), kept_mask)


def forward_rows(row_block, qkv_half, out_half, vec_real, router_half):
    normed_one, inv_one = normalize(row_block)
    attn_in = to_half(normed_one * vec_real[0] + vec_real[1])
    projected = jnp.dot(attn_in, qkv_half, preferred_element_type=jnp.float32)
    queries = to_half((projected[:, :D] + vec_real[4]) * HEAD ** (-0.5))
    keys_b = to_half(projected[:, D : 2 * D])
    values_b = to_half(projected[:, 2 * D :] + vec_real[5])
    scores = jnp.einsum(
        "ishd,ithd->ihst",
        heads_split(queries),
        heads_split(keys_b),
        preferred_element_type=jnp.float32,
    )
    log_total = jnp.log(jnp.sum(jnp.exp(scores), axis=-1))
    prob_half = to_half(jnp.exp(scores - log_total[..., None]))
    head_mix = to_half(
        jnp.einsum(
            "ihst,ithd->ishd", prob_half, heads_split(values_b), preferred_element_type=jnp.float32
        ).reshape(-1, D)
    )
    hidden_res = (
        row_block + jnp.dot(head_mix, out_half, preferred_element_type=jnp.float32) + vec_real[6]
    )
    normed_two, inv_two = normalize(hidden_res)
    moe_in = to_half(normed_two * vec_real[2] + vec_real[3])
    exp_logit = jnp.exp(
        jnp.einsum("td,ed->te", moe_in, router_half, preferred_element_type=jnp.float32)
    )
    route_prob = exp_logit / jnp.sum(exp_logit, axis=-1, keepdims=True)
    return (
        attn_in,
        normed_one,
        inv_one,
        queries,
        keys_b,
        values_b,
        log_total,
        head_mix,
        hidden_res,
        normed_two,
        inv_two,
        moe_in,
        route_prob,
    )


def backward_rows(
    saved, grad_moe, cot_rows, grad_gate, ids_here, qkv_half, out_half, vec_real, router_half
):
    (
        attn_in,
        normed_one,
        inv_one,
        queries,
        keys_b,
        values_b,
        log_total,
        head_mix,
        hidden_res,
        normed_two,
        inv_two,
        moe_in,
        route_prob,
    ) = saved
    onehot = expert_table(ids_here)
    grad_prob = jnp.sum(grad_gate[..., None] * onehot, axis=1)
    grad_logit = route_prob * (grad_prob - jnp.sum(route_prob * grad_prob, axis=-1, keepdims=True))
    logit_half = to_half(grad_logit)
    router_grad = jnp.einsum("te,td->ed", logit_half, moe_in, preferred_element_type=jnp.float32)
    grad_moe = grad_moe + jnp.dot(logit_half, router_half, preferred_element_type=jnp.float32)
    gain_two = jnp.sum(grad_moe * normed_two, axis=0)
    shift_two = jnp.sum(grad_moe, axis=0)
    grad_res = cot_rows + normalize_back(grad_moe * vec_real[2], normed_two, inv_two)
    res_half = to_half(grad_res)
    bias_out = jnp.sum(grad_res, axis=0)
    out_part = jnp.einsum("tf,td->fd", head_mix, res_half, preferred_element_type=jnp.float32)
    grad_mix = to_half(
        jnp.einsum("td,fd->tf", res_half, out_half, preferred_element_type=jnp.float32)
    )
    scores = jnp.einsum(
        "ishd,ithd->ihst",
        heads_split(queries),
        heads_split(keys_b),
        preferred_element_type=jnp.float32,
    )
    prob_full = jnp.exp(scores - log_total[..., None])
    prob_half = to_half(prob_full)
    grad_probs = jnp.einsum(
        "ishd,ithd->ihst",
        heads_split(grad_mix),
        heads_split(values_b),
        preferred_element_type=jnp.float32,
    )
    grad_values = jnp.einsum(
        "ihst,ishd->ithd", prob_half, heads_split(grad_mix), preferred_element_type=jnp.float32
    )
    grad_scores = prob_full * (grad_probs - jnp.sum(prob_full * grad_probs, axis=-1, keepdims=True))
    score_half = to_half(grad_scores)
    grad_queries = jnp.einsum(
        "ihst,ithd->ishd", score_half, heads_split(keys_b), preferred_element_type=jnp.float32
    ) * HEAD ** (-0.5)
    grad_keys = jnp.einsum(
        "ihst,ishd->ithd", score_half, heads_split(queries), preferred_element_type=jnp.float32
    )
    grad_queries = grad_queries.reshape(-1, D)
    grad_values = grad_values.reshape(-1, D)
    proj_half = to_half(
        jnp.concatenate([grad_queries, grad_keys.reshape(-1, D), grad_values], axis=1)
    )
    qkv_part = jnp.einsum("td,tq->dq", attn_in, proj_half, preferred_element_type=jnp.float32)
    grad_attn = jnp.einsum("tq,dq->td", proj_half, qkv_half, preferred_element_type=jnp.float32)
    gain_one = jnp.sum(grad_attn * normed_one, axis=0)
    shift_one = jnp.sum(grad_attn, axis=0)
    grad_rows = grad_res + normalize_back(grad_attn * vec_real[0], normed_one, inv_one)
    small_part = jnp.stack(
        [
            gain_one,
            shift_one,
            gain_two,
            shift_two,
            jnp.sum(grad_queries, axis=0),
            jnp.sum(grad_values, axis=0),
            bias_out,
        ]
    )
    return (grad_rows, qkv_part, out_part, small_part, router_grad)


def adamw_step(weight, grad, first_m, second_m):
    new_first = BETA_ONE * first_m + (1.0 - BETA_ONE) * grad
    new_second = BETA_TWO * second_m + (1.0 - BETA_TWO) * grad * grad
    step_dir = new_first / CORR_ONE / (jnp.sqrt(new_second / CORR_TWO) + ADAM_EPS)
    return (weight - LEARN_RATE * (step_dir + WEIGHT_DECAY * weight), new_first, new_second)


def body_any(
    tokens,
    cotangent,
    expert_ids,
    slot_pos,
    qkv_w,
    qkv_m,
    qkv_v,
    out_w,
    out_m,
    out_v,
    vectors,
    vec_m,
    vec_v,
    w_in,
    w_in_m,
    w_in_v,
    w_out,
    w_out_m,
    w_out_v,
    b_in,
    b_in_m,
    b_in_v,
):
    qkv_shard = to_half(qkv_w)
    out_shard = to_half(out_w)
    vec_shard = to_half(vectors)
    qkv_half, out_half, vec_half = (
        lax.all_gather(qkv_shard, ("dp", "group"), axis=0, tiled=True),
        lax.all_gather(out_shard, ("dp", "group"), axis=0, tiled=True),
        lax.all_gather(vec_shard, ("dp", "group"), axis=1, tiled=True),
    )
    win_full, wout_full, bin_full = (
        lax.all_gather(to_half(w_in), "group", axis=0, tiled=True),
        lax.all_gather(to_half(w_out), "group", axis=1, tiled=True),
        lax.all_gather(to_half(b_in), "group", axis=0, tiled=True),
    )
    vec_real = vec_half.astype(jnp.float32)
    router_half = vec_half[7 : 7 + EXPERTS]
    out_bias = vec_real[7 + EXPERTS :]
    hid_cols = win_full.shape[1]
    local_exp = max(1, hid_cols // FF)
    hid_width = hid_cols // local_exp
    split_count = FF // hid_width
    dp_count = lax.axis_size("dp")
    weight_in = win_full.reshape(D, local_exp, hid_width).transpose(1, 0, 2)
    weight_out = wout_full.reshape(local_exp, hid_width, D)
    bias_in = bin_full.astype(jnp.float32).reshape(local_exp, hid_width)

    def spread(buffer):
        return jnp.repeat(buffer.reshape(EXPERTS, CAP, D), split_count, axis=0)

    def to_experts(arrived):
        return (
            arrived.reshape(dp_count, local_exp, CAP, D)
            .transpose(1, 0, 2, 3)
            .reshape(local_exp, dp_count * CAP, D)
        )

    def to_sources(expert_rows):
        return (
            expert_rows.reshape(local_exp, dp_count, CAP, D)
            .transpose(1, 0, 2, 3)
            .reshape(dp_count * local_exp, CAP, D)
        )

    def join_parts(arrived):
        return jnp.sum(arrived.reshape(EXPERTS, split_count, CAP, D), axis=1).reshape(
            EXPERTS * CAP, D
        )

    saved = forward_rows(tokens, qkv_half, out_half, vec_real, router_half)
    slot_hits, kept_mask = slot_table(expert_ids, slot_pos)
    packed = to_half(
        jnp.einsum(
            "ts,td->sd",
            to_half(jnp.sum(slot_hits, axis=1)),
            saved[11],
            preferred_element_type=jnp.float32,
        )
    )
    routed_rows = to_experts(
        lax.all_to_all(spread(packed), "dp", split_axis=0, concat_axis=0, tiled=True)
    )
    pre_act = (
        jnp.einsum("erd,edh->erh", routed_rows, weight_in, preferred_element_type=jnp.float32)
        + bias_in[:, None, :]
    )
    expert_res = jnp.einsum(
        "erh,ehd->erd",
        to_half(jax.nn.gelu(pre_act)),
        weight_out,
        preferred_element_type=jnp.float32,
    )
    combined = join_parts(
        lax.all_to_all(
            to_sources(expert_res).astype(jnp.bfloat16),
            "dp",
            split_axis=0,
            concat_axis=0,
            tiled=True,
        ).astype(jnp.float32)
    )
    chosen, kept_mask = select_rows(combined, expert_ids, slot_pos)
    onehot = expert_table(expert_ids)
    chosen = chosen + jnp.einsum("tke,ed->tkd", onehot, out_bias, precision=EXACT)
    gate_vals = jnp.where(kept_mask, jnp.take_along_axis(saved[12], expert_ids, axis=1), 0.0)
    block_out = saved[8] + jnp.sum(gate_vals[..., None] * chosen, axis=1)
    grad_gate = jnp.where(kept_mask, jnp.sum(cotangent[:, None, :] * chosen, axis=-1), 0.0)
    weighted = gate_vals[..., None] * cotangent[:, None, :]
    grad_packed = to_half(jnp.einsum("tks,tkd->sd", slot_hits, weighted, precision=EXACT))
    bias_grad = jnp.einsum("tke,tkd->ed", onehot, weighted, precision=EXACT)
    grad_routed = to_experts(
        lax.all_to_all(spread(grad_packed), "dp", split_axis=0, concat_axis=0, tiled=True)
    )
    activated, gelu_back = jax.vjp(jax.nn.gelu, pre_act)
    act_half = to_half(activated)
    grad_act = jnp.einsum(
        "erd,ehd->erh", grad_routed, weight_out, preferred_element_type=jnp.float32
    )
    grad_wout = jnp.einsum(
        "erh,erd->ehd", act_half, grad_routed, preferred_element_type=jnp.float32
    )
    grad_pre = gelu_back(grad_act)[0]
    grad_bias_in = jnp.sum(grad_pre, axis=1)
    pre_half = to_half(grad_pre)
    grad_win = jnp.einsum("erd,erh->edh", routed_rows, pre_half, preferred_element_type=jnp.float32)
    grad_inputs = jnp.einsum(
        "erh,edh->erd", pre_half, weight_in, preferred_element_type=jnp.float32
    )
    slot_grads = join_parts(
        lax.all_to_all(
            to_sources(grad_inputs).astype(jnp.bfloat16),
            "dp",
            split_axis=0,
            concat_axis=0,
            tiled=True,
        ).astype(jnp.float32)
    )
    w_in_grad, w_out_grad, b_in_grad = (
        lax.psum_scatter(
            grad_win.transpose(1, 0, 2).reshape(D, hid_cols).astype(jnp.bfloat16),
            "group",
            scatter_dimension=0,
            tiled=True,
        ).astype(jnp.float32),
        lax.psum_scatter(
            grad_wout.reshape(hid_cols, D).astype(jnp.bfloat16),
            "group",
            scatter_dimension=1,
            tiled=True,
        ).astype(jnp.float32),
        lax.psum_scatter(
            grad_bias_in.reshape(hid_cols).astype(jnp.bfloat16),
            "group",
            scatter_dimension=0,
            tiled=True,
        ).astype(jnp.float32),
    )
    picked, kept_mask = select_rows(slot_grads, expert_ids, slot_pos)
    grad_moe = jnp.sum(jnp.where(kept_mask[..., None], picked, 0.0), axis=1)
    input_grad, qkv_part, out_part, small_part, router_grad = backward_rows(
        saved, grad_moe, cotangent, grad_gate, expert_ids, qkv_half, out_half, vec_real, router_half
    )
    vec_part = jnp.concatenate([small_part, router_grad, bias_grad], axis=0)
    qkv_grad, out_grad, vec_grad = (
        lax.psum_scatter(qkv_part, ("dp", "group"), scatter_dimension=0, tiled=True),
        lax.psum_scatter(out_part, ("dp", "group"), scatter_dimension=0, tiled=True),
        lax.psum_scatter(vec_part, ("dp", "group"), scatter_dimension=1, tiled=True),
    )
    branch_bias_grad = jnp.concatenate([vec_grad[6:7], vec_grad[7 + EXPERTS :]], axis=0)
    qkv_new, qkv_m_new, qkv_v_new = adamw_step(qkv_w, qkv_grad, qkv_m, qkv_v)
    out_new, out_m_new, out_v_new = adamw_step(out_w, out_grad, out_m, out_v)
    vec_new, vec_m_new, vec_v_new = adamw_step(vectors, vec_grad, vec_m, vec_v)
    w_in_new, w_in_m_new, w_in_v_new = adamw_step(w_in, w_in_grad, w_in_m, w_in_v)
    w_out_new, w_out_m_new, w_out_v_new = adamw_step(w_out, w_out_grad, w_out_m, w_out_v)
    b_in_new, b_in_m_new, b_in_v_new = adamw_step(b_in, b_in_grad, b_in_m, b_in_v)
    return (
        block_out,
        input_grad,
        qkv_grad,
        qkv_new,
        qkv_m_new,
        qkv_v_new,
        out_grad,
        out_new,
        out_m_new,
        out_v_new,
        vec_grad,
        vec_new,
        vec_m_new,
        vec_v_new,
        w_in_grad,
        w_in_new,
        w_in_m_new,
        w_in_v_new,
        w_out_grad,
        w_out_new,
        w_out_m_new,
        w_out_v_new,
        b_in_grad,
        b_in_new,
        b_in_m_new,
        b_in_v_new,
        branch_bias_grad,
    )


AXES = ("y", "x", "core", "group")
CHIPS = ("y", "x", "group")
COLUMN = ("core", "group")
SWAP = [(0, 1), (1, 0)]
WIDE = 3200
SHARD = 24


def exact_dot(left, right, dims):
    return lax.dot_general(left, right, (dims, ((), ())), preferred_element_type=jnp.float32)


def shift_perm(step):
    return [(i, (i + step) % 4) for i in range(4)]


def place():
    return tuple(lax.axis_index(name) for name in AXES)


def join_swap(rows, axis_name):
    return jnp.concatenate([rows, lax.ppermute(rows, axis_name, SWAP)], axis=0)


def gather_line(shard):
    return [shard] + [lax.ppermute(shard, "group", shift_perm(step)) for step in (1, 2, 3)]


def fold_swap(rows, axis_name):
    half = rows.shape[0] // 2
    arrived = lax.ppermute(rows[half:], axis_name, SWAP)
    return to_half(rows[:half].astype(jnp.float32) + arrived.astype(jnp.float32))


def row_order():
    row_y, row_x, core, line = place()
    spot = jnp.arange(D)
    half = spot // 384
    other = (spot // 192) % 2
    outer = (spot // 96) % 2
    inner = (spot // 48) % 2
    step = half * 2 + (spot // SHARD) % 2
    y_rel = jnp.where(half == 0, outer, inner)
    x_rel = jnp.where(half == 0, inner, outer)
    owner = (((row_y ^ y_rel) * 2 + (row_x ^ x_rel)) * 2 + (core ^ other)) * 4 + (line - step) % 4
    feature = owner * SHARD + spot % SHARD
    return to_half(feature[:, None] == jnp.arange(D)[None, :])


def column_pairs(turn):
    pairs = []
    for core in range(2):
        for line in range(4):
            part = (line + turn) % 4
            pairs.append((core * 4 + line, (part % 2) * 4 + 2 * core + part // 2))
    return pairs


def host_parts(rows):
    row_y, row_x, core, line = place()
    width = rows.shape[1] // 4
    return [
        to_half(lax.dynamic_slice_in_dim(rows, (line + turn) % 4 * width, width, axis=1))
        for turn in range(4)
    ]


def to_host(part, turn):
    return lax.ppermute(part, COLUMN, column_pairs(turn))


def settle(arrived):
    row_y, row_x, core, line = place()
    stacked = jnp.stack(arrived, axis=0)
    here = 2 * (line % 2) + core
    pieces = [
        lax.dynamic_index_in_dim(stacked, (here - piece) % 4, axis=0, keepdims=False)
        for piece in range(4)
    ]
    return jnp.concatenate(pieces, axis=0)


def owner_pieces(grads):
    row_y, row_x, core, line = place()
    here = 2 * (line % 2) + core
    pieces = to_half(grads).reshape(4, -1, grads.shape[1])
    return [
        lax.dynamic_index_in_dim(pieces, (here - turn) % 4, axis=0, keepdims=False)
        for turn in range(4)
    ]


def to_owner(piece, turn):
    return lax.ppermute(piece, COLUMN, [(host, owner) for owner, host in column_pairs(turn)])


def after(gate, *values):
    return lax.optimization_barrier((gate, *values))


def to_owners_end(arrived):
    row_y, row_x, core, line = place()
    stacked = jnp.stack(arrived, axis=0)
    parts = [
        lax.dynamic_index_in_dim(stacked, (part - line) % 4, axis=0, keepdims=False)
        for part in range(4)
    ]
    return jnp.concatenate(parts, axis=1).astype(jnp.float32)


ROWS = 256
LANES = 128
VMEM_BYTES = 56 * 1024 * 1024


def pair_masks(shape):
    lane = lax.broadcasted_iota(jnp.int32, shape, 1)
    return lane < HEAD, lane >= HEAD


def dot_nt(left, right):
    return exact_dot(left, right, ((1,), (1,)))


def dot_nn(left, right):
    return exact_dot(left, right, ((1,), (0,)))


def dot_tn(left, right):
    return exact_dot(left, right, ((0,), (0,)))


def only(mask, values):
    return jnp.where(mask, values, jnp.zeros_like(values))


def slot_hit(target, count):
    return to_half(target == lax.broadcasted_iota(jnp.int32, (target.shape[0], count), 1))


def attend_kernel(
    tokens_ref,
    cot_ref,
    weights_ref,
    order_ref,
    ids_ref,
    slots_ref,
    attn_rel_ref,
    queries_ref,
    keys_ref,
    values_ref,
    log_ref,
    mix_rel_ref,
    hidden_ref,
    moe_ref,
    prob_ref,
    vec_ref,
    bias_ref,
    send_ref,
    mix_ref,
):
    f32 = jnp.float32
    order = order_ref[...]
    vec = dot_tn(weights_ref[:, 4 * D :], order)
    vec_ref[...] = vec
    tokens = tokens_ref[...]
    normed_one, inv_one = normalize(tokens)
    attn_in = to_half(normed_one * vec[0:1] + vec[1:2])
    attn_rel = to_half(dot_nt(attn_in, order))
    attn_rel_ref[...] = attn_rel
    queries_ref[...] = to_half(
        (dot_nn(attn_rel, weights_ref[:, :D]) + vec[4:5]) * HEAD ** (-0.5)
    )
    keys_ref[...] = to_half(dot_nn(attn_rel, weights_ref[:, D : 2 * D]))
    values_ref[...] = to_half(dot_nn(attn_rel, weights_ref[:, 2 * D : 3 * D]) + vec[5:6])
    masks = pair_masks((ROWS, LANES))
    real = lax.broadcasted_iota(jnp.int32, (ROWS, ROWS), 1) < SEQ
    lane = lax.broadcasted_iota(jnp.int32, (ROWS, LANES), 1)
    logs = jnp.zeros((ROWS, LANES), f32)
    for pair in range(HEADS // 2):
        cols = slice(pair * LANES, (pair + 1) * LANES)
        queries, keys, values = queries_ref[:, cols], keys_ref[:, cols], values_ref[:, cols]
        mixed = jnp.zeros((ROWS, LANES), f32)
        for side in range(2):
            scores = dot_nt(queries, only(masks[side], keys))
            powers = jnp.where(real, jnp.exp(scores), 0.0)
            log_total = jnp.log(jnp.sum(powers, axis=-1, keepdims=True))
            prob = jnp.where(real, jnp.exp(scores - log_total), 0.0)
            mixed = mixed + dot_nn(to_half(prob), only(masks[side], values))
            logs = jnp.where(lane == 2 * pair + side, log_total, logs)
        mix_ref[:, cols] = to_half(mixed)
    log_ref[...] = logs
    mix_rel = to_half(dot_nt(mix_ref[...], order))
    mix_rel_ref[...] = mix_rel
    hidden = tokens + dot_nn(mix_rel, weights_ref[:, 3 * D : 4 * D]) + vec[6:7]
    hidden_ref[...] = hidden
    normed_two, inv_two = normalize(hidden)
    moe_in = to_half(normed_two * vec[2:3] + vec[3:4])
    moe_ref[...] = moe_in
    logits = dot_nt(moe_in, to_half(vec))
    routed = (lane >= 7) & (lane < 7 + EXPERTS)
    exp_logit = jnp.where(routed, jnp.exp(jnp.where(routed, logits, 0.0)), 0.0)
    prob = exp_logit / jnp.sum(exp_logit, axis=-1, keepdims=True)
    prob_ref[...] = prob
    cot = cot_ref[...]
    hits, weighted, gates = [], [], jnp.zeros((ROWS, LANES), f32)
    for k in range(2):
        ids, slots = ids_ref[:, k : k + 1], slots_ref[:, k : k + 1]
        here = (lane == ids + 7) & (slots >= 0)
        gate = jnp.sum(jnp.where(here, prob, 0.0), axis=-1, keepdims=True)
        gates = gates + jnp.where(lane == ids + 7 + EXPERTS, gate, 0.0)
        hits.append(slot_hit(jnp.where(slots >= 0, ids * CAP + slots, -1), EXPERTS * CAP))
        weighted.append(to_half(gate * cot))
    bias_ref[...] = lax.dot_general(
        gates, cot, (((0,), (0,)), ((), ())), precision=EXACT, preferred_element_type=f32
    )
    send_ref[:, :D] = to_half(dot_tn(hits[0] + hits[1], moe_in))
    send_ref[:, D:] = to_half(dot_tn(hits[0], weighted[0]) + dot_tn(hits[1], weighted[1]))


def retreat_kernel(
    tokens_ref,
    cot_ref,
    weights_ref,
    order_ref,
    ids_ref,
    slots_ref,
    attn_rel_ref,
    queries_ref,
    keys_ref,
    values_ref,
    log_ref,
    mix_rel_ref,
    hidden_ref,
    moe_ref,
    prob_ref,
    vec_ref,
    bias_ref,
    returned_ref,
    block_ref,
    input_ref,
    rows_ref,
    grad_mix_ref,
    proj_ref,
):
    f32 = jnp.float32
    order = order_ref[...]
    vec = vec_ref[...]
    vec_half = to_half(vec)
    cot = cot_ref[...]
    hidden = hidden_ref[...]
    prob = prob_ref[...]
    lane = lax.broadcasted_iota(jnp.int32, (ROWS, LANES), 1)
    block_out = hidden
    grad_prob = jnp.zeros((ROWS, LANES), f32)
    grad_moe = jnp.zeros((ROWS, D), f32)
    for k in range(2):
        ids, slots = ids_ref[:, k : k + 1], slots_ref[:, k : k + 1]
        kept = slots >= 0
        mine = lane == ids + 7
        gate = jnp.sum(jnp.where(mine & kept, prob, 0.0), axis=-1, keepdims=True)
        hits = slot_hit(jnp.where(kept, ids * CAP + slots, -1), EXPERTS * CAP)
        bias_hit = to_half(lane == ids + 7 + EXPERTS)
        chosen = dot_nn(hits, returned_ref[:, :D]) + dot_nn(bias_hit, vec_half)
        block_out = block_out + gate * chosen
        grad_gate = jnp.where(kept, jnp.sum(cot * chosen, axis=-1, keepdims=True), 0.0)
        grad_prob = grad_prob + jnp.where(mine, grad_gate, 0.0)
        grad_moe = grad_moe + dot_nn(hits, returned_ref[:, D:])
    block_ref[...] = block_out[:SEQ]
    grad_logit = prob * (grad_prob - jnp.sum(prob * grad_prob, axis=-1, keepdims=True))
    logit_half = to_half(grad_logit)
    router_grad = dot_tn(logit_half, moe_ref[...])
    grad_moe = grad_moe + dot_nn(logit_half, vec_half)
    normed_two, inv_two = normalize(hidden)
    gain_two = jnp.sum(grad_moe * normed_two, axis=0, keepdims=True)
    shift_two = jnp.sum(grad_moe, axis=0, keepdims=True)
    grad_res = cot + normalize_back(grad_moe * vec[2:3], normed_two, inv_two)
    res_half = to_half(grad_res)
    bias_out = jnp.sum(grad_res, axis=0, keepdims=True)
    rows_ref[:, 3 * D : 4 * D] = to_half(dot_tn(mix_rel_ref[...], res_half))
    mix_back = to_half(dot_nt(res_half, weights_ref[:, 3 * D : 4 * D]))
    grad_mix_ref[...] = to_half(dot_nn(mix_back, order))
    masks = pair_masks((ROWS, LANES))
    real = lax.broadcasted_iota(jnp.int32, (ROWS, ROWS), 1) < SEQ
    logs = log_ref[...]
    query_sums, value_sums = [], []
    for pair in range(HEADS // 2):
        cols = slice(pair * LANES, (pair + 1) * LANES)
        queries, keys, values = queries_ref[:, cols], keys_ref[:, cols], values_ref[:, cols]
        grad_mix = grad_mix_ref[:, cols]
        grad_q = jnp.zeros((ROWS, LANES), f32)
        grad_k = jnp.zeros((ROWS, LANES), f32)
        grad_v = jnp.zeros((ROWS, LANES), f32)
        for side in range(2):
            keys_one = only(masks[side], keys)
            log_total = jnp.sum(
                jnp.where(lane == 2 * pair + side, logs, 0.0), axis=-1, keepdims=True
            )
            probs = jnp.where(real, jnp.exp(dot_nt(queries, keys_one) - log_total), 0.0)
            grad_probs = dot_nt(grad_mix, only(masks[side], values))
            grad_scores = probs * (
                grad_probs - jnp.sum(probs * grad_probs, axis=-1, keepdims=True)
            )
            score_half = to_half(grad_scores)
            grad_q = grad_q + dot_nn(score_half, keys_one)
            grad_k = grad_k + dot_tn(score_half, only(masks[side], queries))
            grad_v = grad_v + dot_tn(to_half(probs), only(masks[side], grad_mix))
        grad_q = grad_q * HEAD ** (-0.5)
        proj_ref[:, cols] = to_half(grad_q)
        proj_ref[:, D + pair * LANES : D + (pair + 1) * LANES] = to_half(grad_k)
        proj_ref[:, 2 * D + pair * LANES : 2 * D + (pair + 1) * LANES] = to_half(grad_v)
        query_sums.append(jnp.sum(grad_q, axis=0, keepdims=True))
        value_sums.append(jnp.sum(grad_v, axis=0, keepdims=True))
    attn_rel = attn_rel_ref[...]
    for part in range(3):
        cols = slice(part * D, (part + 1) * D)
        rows_ref[:, cols] = to_half(dot_tn(attn_rel, proj_ref[:, cols]))
    attn_back = dot_nt(proj_ref[...], weights_ref[:, : 3 * D])
    grad_attn = lax.dot_general(
        attn_back,
        order.astype(f32),
        (((1,), (0,)), ((), ())),
        precision=EXACT,
        preferred_element_type=f32,
    )
    normed_one, inv_one = normalize(tokens_ref[...])
    gain_one = jnp.sum(grad_attn * normed_one, axis=0, keepdims=True)
    shift_one = jnp.sum(grad_attn, axis=0, keepdims=True)
    input_grad = grad_res + normalize_back(grad_attn * vec[0:1], normed_one, inv_one)
    input_ref[...] = input_grad[:SEQ]
    table = lax.broadcasted_iota(jnp.int32, (LANES, D), 0)
    vec_part = router_grad + bias_ref[...]
    small = [
        gain_one,
        shift_one,
        gain_two,
        shift_two,
        jnp.concatenate(query_sums, axis=1),
        jnp.concatenate(value_sums, axis=1),
        bias_out,
    ]
    for row, values in enumerate(small):
        vec_part = jnp.where(table == row, values, vec_part)
    rows_ref[:, 4 * D :] = to_half(dot_nt(order, to_half(vec_part)))


def whole_call(kernel, outs, scratch, flops, args):
    return pl.pallas_call(
        kernel,
        out_shape=[jax.ShapeDtypeStruct(shape, dtype) for shape, dtype in outs],
        in_specs=[pl.BlockSpec(memory_space=pltpu.VMEM)] * len(args),
        out_specs=[pl.BlockSpec(memory_space=pltpu.VMEM)] * len(outs),
        scratch_shapes=[pltpu.VMEM(shape, dtype) for shape, dtype in scratch],
        compiler_params=pltpu.CompilerParams(vmem_limit_bytes=VMEM_BYTES),
        cost_estimate=pl.CostEstimate(flops=flops, bytes_accessed=1 << 24, transcendentals=1 << 20),
    )(*args)


BIAS_PAIRS = [(i, (i % 2) * 4 + i // 2) for i in range(8)]


def body_column(
    tokens,
    cotangent,
    expert_ids,
    slot_pos,
    qkv_w,
    qkv_m,
    qkv_v,
    out_w,
    out_m,
    out_v,
    vectors,
    vec_m,
    vec_v,
    w_in,
    w_in_m,
    w_in_v,
    w_out,
    w_out_m,
    w_out_v,
    b_in,
    b_in_m,
    b_in_v,
):
    f32 = jnp.float32
    shard = jnp.concatenate(
        [
            to_half(qkv_w),
            to_half(out_w),
            jnp.pad(to_half(vectors.T), ((0, 0), (0, WIDE - 4 * D - vectors.shape[0]))),
        ],
        axis=1,
    )
    bias_in = lax.ppermute(to_half(b_in), COLUMN, BIAS_PAIRS)
    blocks = gather_line(shard)
    win_parts = host_parts(w_in)
    wout_parts = host_parts(w_out.T)
    blocks, win_parts, bias_in = after(blocks, win_parts, bias_in)
    bias_in = bias_in.astype(f32)
    win_parts = [to_host(part, turn) for turn, part in enumerate(win_parts)]
    first = jnp.concatenate(blocks[:2], axis=0)
    second = jnp.concatenate(blocks[2:], axis=0)
    first, second = join_swap(first, "x"), join_swap(second, "y")
    first, second, win_parts[0] = after(first, second, win_parts[0])
    first, second = join_swap(first, "y"), join_swap(second, "x")
    first, second, win_parts[1] = after(first, second, win_parts[1])
    gathered = jnp.concatenate([join_swap(first, "core"), join_swap(second, "core")], axis=0)

    pad = ((0, ROWS - SEQ), (0, 0))
    shared = (
        jnp.pad(tokens, pad),
        jnp.pad(cotangent, pad),
        gathered,
        row_order(),
        jnp.pad(expert_ids, pad),
        jnp.pad(slot_pos, pad, constant_values=-1),
    )
    half = jnp.bfloat16
    *kept, sent = whole_call(
        attend_kernel,
        [((ROWS, D), half)] * 4
        + [((ROWS, LANES), f32), ((ROWS, D), half), ((ROWS, D), f32), ((ROWS, D), half)]
        + [((ROWS, LANES), f32), ((LANES, D), f32), ((LANES, D), f32)]
        + [((EXPERTS * CAP, 2 * D), half)],
        [((ROWS, D), half)],
        6 << 30,
        shared,
    )
    sent, win_parts[2:], wout_parts = after(sent, win_parts[2:], wout_parts)
    wout_parts[:2] = [to_host(wout_parts[turn], turn) for turn in (0, 1)]

    def swap_chips(rows):
        chunks = rows.reshape(EXPERTS, -1, 2 * LANES)
        swapped = lax.all_to_all(chunks, CHIPS, split_axis=0, concat_axis=0, tiled=True)
        return swapped.reshape(rows.shape)

    routed_own = swap_chips(sent)
    routed_own, wout_parts = after(routed_own, wout_parts)
    wout_parts[2:] = [to_host(wout_parts[turn], turn) for turn in (2, 3)]
    routed = jnp.concatenate([routed_own, lax.ppermute(routed_own, "core", SWAP)], axis=0)
    rows_in, grads_in = routed[:, :D], routed[:, D:]

    weight_in = settle(win_parts)
    pre_act = jnp.dot(rows_in, weight_in, preferred_element_type=f32) + bias_in[None, :]
    activated, gelu_back = jax.vjp(jax.nn.gelu, pre_act)
    act_half = to_half(activated)
    grad_wout = exact_dot(grads_in, act_half, ((0,), (0,)))
    wout_back = owner_pieces(grad_wout)
    wout_back[0], wout_parts[:3] = after(wout_back[0], wout_parts[:3])
    wout_back[1], wout_parts[3] = after(wout_back[1], wout_parts[3])
    weight_out = settle(wout_parts)
    expert_res = exact_dot(act_half, weight_out, ((1,), (1,)))
    grad_act = exact_dot(grads_in, weight_out, ((1,), (0,)))
    grad_pre = gelu_back(grad_act)[0]
    grad_bias_in = jnp.sum(grad_pre, axis=0)
    pre_half = to_half(grad_pre)
    grad_win = exact_dot(rows_in, pre_half, ((0,), (0,)))
    grad_slots = exact_dot(pre_half, weight_in, ((1,), (1,)))

    results = jnp.concatenate([expert_res, grad_slots], axis=1)
    there = lax.ppermute(to_half(results[EXPERTS * CAP :]), "core", SWAP)
    sent_back = to_half(results[: EXPERTS * CAP] + there)
    sent_back, wout_back[:2] = after(sent_back, wout_back[:2])
    wout_back[:2] = [to_owner(wout_back[turn], turn) for turn in (0, 1)]
    returned = swap_chips(sent_back)
    win_back = owner_pieces(grad_win)
    block_out, input_grad, rows = whole_call(
        retreat_kernel,
        [((SEQ, D), f32), ((SEQ, D), f32), ((D, WIDE), half)],
        [((ROWS, D), half), ((ROWS, 3 * D), half)],
        12 << 30,
        (*shared, *kept, returned),
    )
    rows, wout_back, win_back = after(rows, wout_back, win_back)
    wout_back[2:] = [to_owner(wout_back[turn], turn) for turn in (2, 3)]
    win_back = [to_owner(piece, turn) for turn, piece in enumerate(win_back)]
    first, second = fold_swap(rows[: D // 2], "core"), fold_swap(rows[D // 2 :], "core")
    first, second, wout_back = after(first, second, wout_back)
    w_out_grad = to_owners_end(wout_back).T
    w_out_all = (w_out_grad, *adamw_step(w_out, w_out_grad, w_out_m, w_out_v))
    first, second = fold_swap(first, "y"), fold_swap(second, "x")
    first, second, win_back[:2] = after(first, second, win_back[:2])
    first, second = fold_swap(first, "x"), fold_swap(second, "y")
    first, second, w_out_all, win_back[2], grad_bias_in = after(
        first, second, w_out_all, win_back[2], grad_bias_in
    )
    w_out_grad, w_out_new, w_out_m_new, w_out_v_new = w_out_all
    w_in_grad = to_owners_end(win_back)
    b_in_grad = lax.ppermute(grad_bias_in, COLUMN, [(host, owner) for owner, host in BIAS_PAIRS])
    blocks = [first[:SHARD], first[SHARD:], second[:SHARD], second[SHARD:]]
    summed = blocks[0].astype(f32)
    for step in (1, 2, 3):
        summed = summed + lax.ppermute(blocks[step], "group", shift_perm(-step)).astype(f32)
    qkv_grad = summed[:, : 3 * D]
    out_grad = summed[:, 3 * D : 4 * D]
    vec_grad = summed[:, 4 * D : 4 * D + vectors.shape[0]].T
    branch_bias_grad = jnp.concatenate([vec_grad[6:7], vec_grad[7 + EXPERTS :]], axis=0)
    qkv_new, qkv_m_new, qkv_v_new = adamw_step(qkv_w, qkv_grad, qkv_m, qkv_v)
    out_new, out_m_new, out_v_new = adamw_step(out_w, out_grad, out_m, out_v)
    vec_new, vec_m_new, vec_v_new = adamw_step(vectors, vec_grad, vec_m, vec_v)
    w_in_new, w_in_m_new, w_in_v_new = adamw_step(w_in, w_in_grad, w_in_m, w_in_v)
    b_in_new, b_in_m_new, b_in_v_new = adamw_step(b_in, b_in_grad, b_in_m, b_in_v)
    return (
        block_out,
        input_grad,
        qkv_grad,
        qkv_new,
        qkv_m_new,
        qkv_v_new,
        out_grad,
        out_new,
        out_m_new,
        out_v_new,
        vec_grad,
        vec_new,
        vec_m_new,
        vec_v_new,
        w_in_grad,
        w_in_new,
        w_in_m_new,
        w_in_v_new,
        w_out_grad,
        w_out_new,
        w_out_m_new,
        w_out_v_new,
        b_in_grad,
        b_in_new,
        b_in_m_new,
        b_in_v_new,
        branch_bias_grad,
    )


def solution(mesh):
    if mesh.shape["dp"] == 8 and mesh.shape["group"] == 4:
        inner = Mesh(mesh.devices.reshape(2, 2, 2, 4), AXES)
        body, dp, group, both = body_column, ("y", "x", "core"), "group", AXES
    else:
        inner, body, dp, group, both = mesh, body_any, "dp", "group", ("dp", "group")
    return jax.shard_map(
        body,
        mesh=inner,
        in_specs=(
            P(both, None),
            P(both, None),
            P(both, None),
            P(both, None),
            P(both, None),
            P(both, None),
            P(both, None),
            P(both, None),
            P(both, None),
            P(both, None),
            P(None, both),
            P(None, both),
            P(None, both),
            P(group, dp),
            P(group, dp),
            P(group, dp),
            P(dp, group),
            P(dp, group),
            P(dp, group),
            P(both),
            P(both),
            P(both),
        ),
        out_specs=(
            P(both, None),
            P(both, None),
            P(both, None),
            P(both, None),
            P(both, None),
            P(both, None),
            P(both, None),
            P(both, None),
            P(both, None),
            P(both, None),
            P(None, both),
            P(None, both),
            P(None, both),
            P(None, both),
            P(group, dp),
            P(group, dp),
            P(group, dp),
            P(group, dp),
            P(dp, group),
            P(dp, group),
            P(dp, group),
            P(dp, group),
            P(both),
            P(both),
            P(both),
            P(both),
            P(None, both),
        ),
        check_vma=False,
    )
```

```python
import jax
import jax.numpy as jnp
from jax import lax
from jax.experimental import pallas as pl
from jax.experimental.pallas import tpu as pltpu
from jax.sharding import Mesh, PartitionSpec as P

D = 768
HEADS = 12
HEAD = 64
FF = 3072
EXPERTS = 16
SEQ = 197
CAP = 25


LEARN_RATE = 0.15
BETA_ONE = 0.9
BETA_TWO = 0.999
ADAM_EPS = 1e-08
WEIGHT_DECAY = 0.1
CORR_ONE = 1.0 - BETA_ONE**2
CORR_TWO = 1.0 - BETA_TWO**2
NORM_EPS = 1e-06
EXACT = lax.Precision.HIGHEST


def to_half(values):
    return values.astype(jnp.bfloat16)


def heads_split(values):
    return values.reshape(-1, SEQ, HEADS, HEAD)


def normalize(values):
    average = jnp.mean(values, axis=-1, keepdims=True)
    centered = values - average
    inv_std = lax.rsqrt(jnp.mean(centered * centered, axis=-1, keepdims=True) + NORM_EPS)
    return (centered * inv_std, inv_std)


def normalize_back(grad_norm, normed, inv_std):
    return inv_std * (
        grad_norm
        - jnp.mean(grad_norm, axis=-1, keepdims=True)
        - normed * jnp.mean(grad_norm * normed, axis=-1, keepdims=True)
    )


def expert_table(ids_here):
    return (ids_here[..., None] == jnp.arange(EXPERTS)[None, None, :]).astype(jnp.float32)


def slot_table(ids_here, slots_here):
    kept_mask = slots_here >= 0
    target = ids_here * CAP + slots_here
    slot_hits = (target[..., None] == jnp.arange(EXPERTS * CAP)[None, None, :]) & kept_mask[
        ..., None
    ]
    return (slot_hits.astype(jnp.float32), kept_mask)


def select_rows(results, ids_here, slots_here):
    kept_mask = slots_here >= 0
    flat_index = jnp.where(kept_mask, ids_here * CAP + slots_here, 0)
    return (jnp.take(results, flat_index, axis=0), kept_mask)


def forward_rows(row_block, qkv_half, out_half, vec_real, router_half):
    normed_one, inv_one = normalize(row_block)
    attn_in = to_half(normed_one * vec_real[0] + vec_real[1])
    projected = jnp.dot(attn_in, qkv_half, preferred_element_type=jnp.float32)
    queries = to_half((projected[:, :D] + vec_real[4]) * HEAD ** (-0.5))
    keys_b = to_half(projected[:, D : 2 * D])
    values_b = to_half(projected[:, 2 * D :] + vec_real[5])
    scores = jnp.einsum(
        "ishd,ithd->ihst",
        heads_split(queries),
        heads_split(keys_b),
        preferred_element_type=jnp.float32,
    )
    log_total = jnp.log(jnp.sum(jnp.exp(scores), axis=-1))
    prob_half = to_half(jnp.exp(scores - log_total[..., None]))
    head_mix = to_half(
        jnp.einsum(
            "ihst,ithd->ishd", prob_half, heads_split(values_b), preferred_element_type=jnp.float32
        ).reshape(-1, D)
    )
    hidden_res = (
        row_block + jnp.dot(head_mix, out_half, preferred_element_type=jnp.float32) + vec_real[6]
    )
    normed_two, inv_two = normalize(hidden_res)
    moe_in = to_half(normed_two * vec_real[2] + vec_real[3])
    exp_logit = jnp.exp(
        jnp.einsum("td,ed->te", moe_in, router_half, preferred_element_type=jnp.float32)
    )
    route_prob = exp_logit / jnp.sum(exp_logit, axis=-1, keepdims=True)
    return (
        attn_in,
        normed_one,
        inv_one,
        queries,
        keys_b,
        values_b,
        log_total,
        head_mix,
        hidden_res,
        normed_two,
        inv_two,
        moe_in,
        route_prob,
    )


def backward_rows(
    saved, grad_moe, cot_rows, grad_gate, ids_here, qkv_half, out_half, vec_real, router_half
):
    (
        attn_in,
        normed_one,
        inv_one,
        queries,
        keys_b,
        values_b,
        log_total,
        head_mix,
        hidden_res,
        normed_two,
        inv_two,
        moe_in,
        route_prob,
    ) = saved
    onehot = expert_table(ids_here)
    grad_prob = jnp.sum(grad_gate[..., None] * onehot, axis=1)
    grad_logit = route_prob * (grad_prob - jnp.sum(route_prob * grad_prob, axis=-1, keepdims=True))
    logit_half = to_half(grad_logit)
    router_grad = jnp.einsum("te,td->ed", logit_half, moe_in, preferred_element_type=jnp.float32)
    grad_moe = grad_moe + jnp.dot(logit_half, router_half, preferred_element_type=jnp.float32)
    gain_two = jnp.sum(grad_moe * normed_two, axis=0)
    shift_two = jnp.sum(grad_moe, axis=0)
    grad_res = cot_rows + normalize_back(grad_moe * vec_real[2], normed_two, inv_two)
    res_half = to_half(grad_res)
    bias_out = jnp.sum(grad_res, axis=0)
    out_part = jnp.einsum("tf,td->fd", head_mix, res_half, preferred_element_type=jnp.float32)
    grad_mix = to_half(
        jnp.einsum("td,fd->tf", res_half, out_half, preferred_element_type=jnp.float32)
    )
    scores = jnp.einsum(
        "ishd,ithd->ihst",
        heads_split(queries),
        heads_split(keys_b),
        preferred_element_type=jnp.float32,
    )
    prob_full = jnp.exp(scores - log_total[..., None])
    prob_half = to_half(prob_full)
    grad_probs = jnp.einsum(
        "ishd,ithd->ihst",
        heads_split(grad_mix),
        heads_split(values_b),
        preferred_element_type=jnp.float32,
    )
    grad_values = jnp.einsum(
        "ihst,ishd->ithd", prob_half, heads_split(grad_mix), preferred_element_type=jnp.float32
    )
    grad_scores = prob_full * (grad_probs - jnp.sum(prob_full * grad_probs, axis=-1, keepdims=True))
    score_half = to_half(grad_scores)
    grad_queries = jnp.einsum(
        "ihst,ithd->ishd", score_half, heads_split(keys_b), preferred_element_type=jnp.float32
    ) * HEAD ** (-0.5)
    grad_keys = jnp.einsum(
        "ihst,ishd->ithd", score_half, heads_split(queries), preferred_element_type=jnp.float32
    )
    grad_queries = grad_queries.reshape(-1, D)
    grad_values = grad_values.reshape(-1, D)
    proj_half = to_half(
        jnp.concatenate([grad_queries, grad_keys.reshape(-1, D), grad_values], axis=1)
    )
    qkv_part = jnp.einsum("td,tq->dq", attn_in, proj_half, preferred_element_type=jnp.float32)
    grad_attn = jnp.einsum("tq,dq->td", proj_half, qkv_half, preferred_element_type=jnp.float32)
    gain_one = jnp.sum(grad_attn * normed_one, axis=0)
    shift_one = jnp.sum(grad_attn, axis=0)
    grad_rows = grad_res + normalize_back(grad_attn * vec_real[0], normed_one, inv_one)
    small_part = jnp.stack(
        [
            gain_one,
            shift_one,
            gain_two,
            shift_two,
            jnp.sum(grad_queries, axis=0),
            jnp.sum(grad_values, axis=0),
            bias_out,
        ]
    )
    return (grad_rows, qkv_part, out_part, small_part, router_grad)


def adamw_step(weight, grad, first_m, second_m):
    new_first = BETA_ONE * first_m + (1.0 - BETA_ONE) * grad
    new_second = BETA_TWO * second_m + (1.0 - BETA_TWO) * grad * grad
    step_dir = new_first / CORR_ONE / (jnp.sqrt(new_second / CORR_TWO) + ADAM_EPS)
    return (weight - LEARN_RATE * (step_dir + WEIGHT_DECAY * weight), new_first, new_second)


def body_any(
    tokens,
    cotangent,
    expert_ids,
    slot_pos,
    qkv_w,
    qkv_m,
    qkv_v,
    out_w,
    out_m,
    out_v,
    vectors,
    vec_m,
    vec_v,
    w_in,
    w_in_m,
    w_in_v,
    w_out,
    w_out_m,
    w_out_v,
    b_in,
    b_in_m,
    b_in_v,
):
    qkv_shard = to_half(qkv_w)
    out_shard = to_half(out_w)
    vec_shard = to_half(vectors)
    qkv_half, out_half, vec_half = (
        lax.all_gather(qkv_shard, ("dp", "group"), axis=0, tiled=True),
        lax.all_gather(out_shard, ("dp", "group"), axis=0, tiled=True),
        lax.all_gather(vec_shard, ("dp", "group"), axis=1, tiled=True),
    )
    win_full, wout_full, bin_full = (
        lax.all_gather(to_half(w_in), "group", axis=0, tiled=True),
        lax.all_gather(to_half(w_out), "group", axis=1, tiled=True),
        lax.all_gather(to_half(b_in), "group", axis=0, tiled=True),
    )
    vec_real = vec_half.astype(jnp.float32)
    router_half = vec_half[7 : 7 + EXPERTS]
    out_bias = vec_real[7 + EXPERTS :]
    hid_cols = win_full.shape[1]
    local_exp = max(1, hid_cols // FF)
    hid_width = hid_cols // local_exp
    split_count = FF // hid_width
    dp_count = lax.axis_size("dp")
    weight_in = win_full.reshape(D, local_exp, hid_width).transpose(1, 0, 2)
    weight_out = wout_full.reshape(local_exp, hid_width, D)
    bias_in = bin_full.astype(jnp.float32).reshape(local_exp, hid_width)

    def spread(buffer):
        return jnp.repeat(buffer.reshape(EXPERTS, CAP, D), split_count, axis=0)

    def to_experts(arrived):
        return (
            arrived.reshape(dp_count, local_exp, CAP, D)
            .transpose(1, 0, 2, 3)
            .reshape(local_exp, dp_count * CAP, D)
        )

    def to_sources(expert_rows):
        return (
            expert_rows.reshape(local_exp, dp_count, CAP, D)
            .transpose(1, 0, 2, 3)
            .reshape(dp_count * local_exp, CAP, D)
        )

    def join_parts(arrived):
        return jnp.sum(arrived.reshape(EXPERTS, split_count, CAP, D), axis=1).reshape(
            EXPERTS * CAP, D
        )

    saved = forward_rows(tokens, qkv_half, out_half, vec_real, router_half)
    slot_hits, kept_mask = slot_table(expert_ids, slot_pos)
    packed = to_half(
        jnp.einsum(
            "ts,td->sd",
            to_half(jnp.sum(slot_hits, axis=1)),
            saved[11],
            preferred_element_type=jnp.float32,
        )
    )
    routed_rows = to_experts(
        lax.all_to_all(spread(packed), "dp", split_axis=0, concat_axis=0, tiled=True)
    )
    pre_act = (
        jnp.einsum("erd,edh->erh", routed_rows, weight_in, preferred_element_type=jnp.float32)
        + bias_in[:, None, :]
    )
    expert_res = jnp.einsum(
        "erh,ehd->erd",
        to_half(jax.nn.gelu(pre_act)),
        weight_out,
        preferred_element_type=jnp.float32,
    )
    combined = join_parts(
        lax.all_to_all(
            to_sources(expert_res).astype(jnp.bfloat16),
            "dp",
            split_axis=0,
            concat_axis=0,
            tiled=True,
        ).astype(jnp.float32)
    )
    chosen, kept_mask = select_rows(combined, expert_ids, slot_pos)
    onehot = expert_table(expert_ids)
    chosen = chosen + jnp.einsum("tke,ed->tkd", onehot, out_bias, precision=EXACT)
    gate_vals = jnp.where(kept_mask, jnp.take_along_axis(saved[12], expert_ids, axis=1), 0.0)
    block_out = saved[8] + jnp.sum(gate_vals[..., None] * chosen, axis=1)
    grad_gate = jnp.where(kept_mask, jnp.sum(cotangent[:, None, :] * chosen, axis=-1), 0.0)
    weighted = gate_vals[..., None] * cotangent[:, None, :]
    grad_packed = to_half(jnp.einsum("tks,tkd->sd", slot_hits, weighted, precision=EXACT))
    bias_grad = jnp.einsum("tke,tkd->ed", onehot, weighted, precision=EXACT)
    grad_routed = to_experts(
        lax.all_to_all(spread(grad_packed), "dp", split_axis=0, concat_axis=0, tiled=True)
    )
    activated, gelu_back = jax.vjp(jax.nn.gelu, pre_act)
    act_half = to_half(activated)
    grad_act = jnp.einsum(
        "erd,ehd->erh", grad_routed, weight_out, preferred_element_type=jnp.float32
    )
    grad_wout = jnp.einsum(
        "erh,erd->ehd", act_half, grad_routed, preferred_element_type=jnp.float32
    )
    grad_pre = gelu_back(grad_act)[0]
    grad_bias_in = jnp.sum(grad_pre, axis=1)
    pre_half = to_half(grad_pre)
    grad_win = jnp.einsum("erd,erh->edh", routed_rows, pre_half, preferred_element_type=jnp.float32)
    grad_inputs = jnp.einsum(
        "erh,edh->erd", pre_half, weight_in, preferred_element_type=jnp.float32
    )
    slot_grads = join_parts(
        lax.all_to_all(
            to_sources(grad_inputs).astype(jnp.bfloat16),
            "dp",
            split_axis=0,
            concat_axis=0,
            tiled=True,
        ).astype(jnp.float32)
    )
    w_in_grad, w_out_grad, b_in_grad = (
        lax.psum_scatter(
            grad_win.transpose(1, 0, 2).reshape(D, hid_cols).astype(jnp.bfloat16),
            "group",
            scatter_dimension=0,
            tiled=True,
        ).astype(jnp.float32),
        lax.psum_scatter(
            grad_wout.reshape(hid_cols, D).astype(jnp.bfloat16),
            "group",
            scatter_dimension=1,
            tiled=True,
        ).astype(jnp.float32),
        lax.psum_scatter(
            grad_bias_in.reshape(hid_cols).astype(jnp.bfloat16),
            "group",
            scatter_dimension=0,
            tiled=True,
        ).astype(jnp.float32),
    )
    picked, kept_mask = select_rows(slot_grads, expert_ids, slot_pos)
    grad_moe = jnp.sum(jnp.where(kept_mask[..., None], picked, 0.0), axis=1)
    input_grad, qkv_part, out_part, small_part, router_grad = backward_rows(
        saved, grad_moe, cotangent, grad_gate, expert_ids, qkv_half, out_half, vec_real, router_half
    )
    vec_part = jnp.concatenate([small_part, router_grad, bias_grad], axis=0)
    qkv_grad, out_grad, vec_grad = (
        lax.psum_scatter(qkv_part, ("dp", "group"), scatter_dimension=0, tiled=True),
        lax.psum_scatter(out_part, ("dp", "group"), scatter_dimension=0, tiled=True),
        lax.psum_scatter(vec_part, ("dp", "group"), scatter_dimension=1, tiled=True),
    )
    branch_bias_grad = jnp.concatenate([vec_grad[6:7], vec_grad[7 + EXPERTS :]], axis=0)
    qkv_new, qkv_m_new, qkv_v_new = adamw_step(qkv_w, qkv_grad, qkv_m, qkv_v)
    out_new, out_m_new, out_v_new = adamw_step(out_w, out_grad, out_m, out_v)
    vec_new, vec_m_new, vec_v_new = adamw_step(vectors, vec_grad, vec_m, vec_v)
    w_in_new, w_in_m_new, w_in_v_new = adamw_step(w_in, w_in_grad, w_in_m, w_in_v)
    w_out_new, w_out_m_new, w_out_v_new = adamw_step(w_out, w_out_grad, w_out_m, w_out_v)
    b_in_new, b_in_m_new, b_in_v_new = adamw_step(b_in, b_in_grad, b_in_m, b_in_v)
    return (
        block_out,
        input_grad,
        qkv_grad,
        qkv_new,
        qkv_m_new,
        qkv_v_new,
        out_grad,
        out_new,
        out_m_new,
        out_v_new,
        vec_grad,
        vec_new,
        vec_m_new,
        vec_v_new,
        w_in_grad,
        w_in_new,
        w_in_m_new,
        w_in_v_new,
        w_out_grad,
        w_out_new,
        w_out_m_new,
        w_out_v_new,
        b_in_grad,
        b_in_new,
        b_in_m_new,
        b_in_v_new,
        branch_bias_grad,
    )


AXES = ("y", "x", "core", "group")
CHIPS = ("y", "x", "group")
COLUMN = ("core", "group")
SWAP = [(0, 1), (1, 0)]
WIDE = 3200
SHARD = 24


def exact_dot(left, right, dims):
    return lax.dot_general(left, right, (dims, ((), ())), preferred_element_type=jnp.float32)


def shift_perm(step):
    return [(i, (i + step) % 4) for i in range(4)]


def place():
    return tuple(lax.axis_index(name) for name in AXES)


def join_swap(rows, axis_name):
    return jnp.concatenate([rows, lax.ppermute(rows, axis_name, SWAP)], axis=0)


def gather_line(shard):
    return [shard] + [lax.ppermute(shard, "group", shift_perm(step)) for step in (1, 2, 3)]


def fold_swap(first, second, first_axis, second_axis):
    half = first.shape[0] // 2
    arrived = (
        lax.ppermute(first[half:], first_axis, SWAP),
        lax.ppermute(second[half:], second_axis, SWAP),
    )
    if first_axis != second_axis:
        arrived = after(*arrived)
    return [
        to_half(own[:half].astype(jnp.float32) + other.astype(jnp.float32))
        for own, other in zip((first, second), arrived)
    ]


def row_order():
    row_y, row_x, core, line = place()
    spot = jnp.arange(D)
    half = spot // 384
    other = (spot // 192) % 2
    outer = (spot // 96) % 2
    inner = (spot // 48) % 2
    step = half * 2 + (spot // SHARD) % 2
    y_rel = jnp.where(half == 0, outer, inner)
    x_rel = jnp.where(half == 0, inner, outer)
    owner = (((row_y ^ y_rel) * 2 + (row_x ^ x_rel)) * 2 + (core ^ other)) * 4 + (line - step) % 4
    feature = owner * SHARD + spot % SHARD
    return to_half(feature[:, None] == jnp.arange(D)[None, :])


def column_pairs(turn):
    pairs = []
    for core in range(2):
        for line in range(4):
            part = (line + turn) % 4
            pairs.append((core * 4 + line, (part % 2) * 4 + 2 * core + part // 2))
    return pairs


def host_parts(rows):
    row_y, row_x, core, line = place()
    width = rows.shape[1] // 4
    return [
        to_half(lax.dynamic_slice_in_dim(rows, (line + turn) % 4 * width, width, axis=1))
        for turn in range(4)
    ]


def to_host(part, turn):
    return lax.ppermute(part, COLUMN, column_pairs(turn))


def settle(arrived):
    row_y, row_x, core, line = place()
    stacked = jnp.stack(arrived, axis=0)
    here = 2 * (line % 2) + core
    pieces = [
        lax.dynamic_index_in_dim(stacked, (here - piece) % 4, axis=0, keepdims=False)
        for piece in range(4)
    ]
    return jnp.concatenate(pieces, axis=0)


def owner_pieces(grads):
    row_y, row_x, core, line = place()
    here = 2 * (line % 2) + core
    pieces = to_half(grads).reshape(4, -1, grads.shape[1])
    return [
        lax.dynamic_index_in_dim(pieces, (here - turn) % 4, axis=0, keepdims=False)
        for turn in range(4)
    ]


def to_owner(piece, turn):
    return lax.ppermute(piece, COLUMN, [(host, owner) for owner, host in column_pairs(turn)])


def after(gate, *values):
    return lax.optimization_barrier((gate, *values))


def to_owners_end(arrived):
    row_y, row_x, core, line = place()
    stacked = jnp.stack(arrived, axis=0)
    parts = [
        lax.dynamic_index_in_dim(stacked, (part - line) % 4, axis=0, keepdims=False)
        for part in range(4)
    ]
    return jnp.concatenate(parts, axis=1).astype(jnp.float32)


ROWS = 256
LANES = 128
VMEM_BYTES = 56 * 1024 * 1024


def pair_masks(shape):
    lane = lax.broadcasted_iota(jnp.int32, shape, 1)
    return lane < HEAD, lane >= HEAD


def dot_nt(left, right):
    return exact_dot(left, right, ((1,), (1,)))


def dot_nn(left, right):
    return exact_dot(left, right, ((1,), (0,)))


def dot_tn(left, right):
    return exact_dot(left, right, ((0,), (0,)))


def only(mask, values):
    return jnp.where(mask, values, jnp.zeros_like(values))


def slot_hit(target, count):
    return to_half(target == lax.broadcasted_iota(jnp.int32, (target.shape[0], count), 1))


def join_pieces(weights_ref, *pieces):
    rows = D // len(pieces)
    for index, piece in enumerate(pieces):
        weights_ref[index * rows : (index + 1) * rows, :] = piece[...]


def attend_kernel(
    tokens_ref,
    cot_ref,
    piece_one,
    piece_two,
    piece_three,
    piece_four,
    order_ref,
    ids_ref,
    slots_ref,
    attn_rel_ref,
    queries_ref,
    keys_ref,
    values_ref,
    log_ref,
    mix_rel_ref,
    hidden_ref,
    moe_ref,
    prob_ref,
    vec_ref,
    bias_ref,
    send_ref,
    mix_ref,
    weights_ref,
):
    f32 = jnp.float32
    join_pieces(weights_ref, piece_one, piece_two, piece_three, piece_four)
    order = order_ref[...]
    vec = dot_tn(weights_ref[:, 4 * D :], order)
    vec_ref[...] = vec
    tokens = tokens_ref[...]
    normed_one, inv_one = normalize(tokens)
    attn_in = to_half(normed_one * vec[0:1] + vec[1:2])
    attn_rel = to_half(dot_nt(attn_in, order))
    attn_rel_ref[...] = attn_rel
    queries_ref[...] = to_half(
        (dot_nn(attn_rel, weights_ref[:, :D]) + vec[4:5]) * HEAD ** (-0.5)
    )
    keys_ref[...] = to_half(dot_nn(attn_rel, weights_ref[:, D : 2 * D]))
    values_ref[...] = to_half(dot_nn(attn_rel, weights_ref[:, 2 * D : 3 * D]) + vec[5:6])
    masks = pair_masks((ROWS, LANES))
    real = lax.broadcasted_iota(jnp.int32, (ROWS, ROWS), 1) < SEQ
    lane = lax.broadcasted_iota(jnp.int32, (ROWS, LANES), 1)
    logs = jnp.zeros((ROWS, LANES), f32)
    for pair in range(HEADS // 2):
        cols = slice(pair * LANES, (pair + 1) * LANES)
        queries, keys, values = queries_ref[:, cols], keys_ref[:, cols], values_ref[:, cols]
        mixed = jnp.zeros((ROWS, LANES), f32)
        for side in range(2):
            scores = dot_nt(queries, only(masks[side], keys))
            powers = jnp.where(real, jnp.exp(scores), 0.0)
            log_total = jnp.log(jnp.sum(powers, axis=-1, keepdims=True))
            prob = jnp.where(real, jnp.exp(scores - log_total), 0.0)
            mixed = mixed + dot_nn(to_half(prob), only(masks[side], values))
            logs = jnp.where(lane == 2 * pair + side, log_total, logs)
        mix_ref[:, cols] = to_half(mixed)
    log_ref[...] = logs
    mix_rel = to_half(dot_nt(mix_ref[...], order))
    mix_rel_ref[...] = mix_rel
    hidden = tokens + dot_nn(mix_rel, weights_ref[:, 3 * D : 4 * D]) + vec[6:7]
    hidden_ref[...] = hidden
    normed_two, inv_two = normalize(hidden)
    moe_in = to_half(normed_two * vec[2:3] + vec[3:4])
    moe_ref[...] = moe_in
    logits = dot_nt(moe_in, to_half(vec))
    routed = (lane >= 7) & (lane < 7 + EXPERTS)
    exp_logit = jnp.where(routed, jnp.exp(jnp.where(routed, logits, 0.0)), 0.0)
    prob = exp_logit / jnp.sum(exp_logit, axis=-1, keepdims=True)
    prob_ref[...] = prob
    cot = cot_ref[...]
    hits, weighted, gates = [], [], jnp.zeros((ROWS, LANES), f32)
    for k in range(2):
        ids, slots = ids_ref[:, k : k + 1], slots_ref[:, k : k + 1]
        here = (lane == ids + 7) & (slots >= 0)
        gate = jnp.sum(jnp.where(here, prob, 0.0), axis=-1, keepdims=True)
        gates = gates + jnp.where(lane == ids + 7 + EXPERTS, gate, 0.0)
        hits.append(slot_hit(jnp.where(slots >= 0, ids * CAP + slots, -1), EXPERTS * CAP))
        weighted.append(to_half(gate * cot))
    bias_ref[...] = lax.dot_general(
        gates, cot, (((0,), (0,)), ((), ())), precision=EXACT, preferred_element_type=f32
    )
    send_ref[:, :D] = to_half(dot_tn(hits[0] + hits[1], moe_in))
    send_ref[:, D:] = to_half(dot_tn(hits[0], weighted[0]) + dot_tn(hits[1], weighted[1]))


def retreat_kernel(
    tokens_ref,
    cot_ref,
    piece_one,
    piece_two,
    piece_three,
    piece_four,
    order_ref,
    ids_ref,
    slots_ref,
    attn_rel_ref,
    queries_ref,
    keys_ref,
    values_ref,
    log_ref,
    mix_rel_ref,
    hidden_ref,
    moe_ref,
    prob_ref,
    vec_ref,
    bias_ref,
    returned_ref,
    block_ref,
    input_ref,
    rows_ref,
    grad_mix_ref,
    proj_ref,
    weights_ref,
):
    f32 = jnp.float32
    join_pieces(weights_ref, piece_one, piece_two, piece_three, piece_four)
    order = order_ref[...]
    vec = vec_ref[...]
    vec_half = to_half(vec)
    cot = cot_ref[...]
    hidden = hidden_ref[...]
    prob = prob_ref[...]
    lane = lax.broadcasted_iota(jnp.int32, (ROWS, LANES), 1)
    block_out = hidden
    grad_prob = jnp.zeros((ROWS, LANES), f32)
    grad_moe = jnp.zeros((ROWS, D), f32)
    for k in range(2):
        ids, slots = ids_ref[:, k : k + 1], slots_ref[:, k : k + 1]
        kept = slots >= 0
        mine = lane == ids + 7
        gate = jnp.sum(jnp.where(mine & kept, prob, 0.0), axis=-1, keepdims=True)
        hits = slot_hit(jnp.where(kept, ids * CAP + slots, -1), EXPERTS * CAP)
        bias_hit = to_half(lane == ids + 7 + EXPERTS)
        chosen = dot_nn(hits, returned_ref[:, :D]) + dot_nn(bias_hit, vec_half)
        block_out = block_out + gate * chosen
        grad_gate = jnp.where(kept, jnp.sum(cot * chosen, axis=-1, keepdims=True), 0.0)
        grad_prob = grad_prob + jnp.where(mine, grad_gate, 0.0)
        grad_moe = grad_moe + dot_nn(hits, returned_ref[:, D:])
    block_ref[...] = block_out[:SEQ]
    grad_logit = prob * (grad_prob - jnp.sum(prob * grad_prob, axis=-1, keepdims=True))
    logit_half = to_half(grad_logit)
    router_grad = dot_tn(logit_half, moe_ref[...])
    grad_moe = grad_moe + dot_nn(logit_half, vec_half)
    normed_two, inv_two = normalize(hidden)
    gain_two = jnp.sum(grad_moe * normed_two, axis=0, keepdims=True)
    shift_two = jnp.sum(grad_moe, axis=0, keepdims=True)
    grad_res = cot + normalize_back(grad_moe * vec[2:3], normed_two, inv_two)
    res_half = to_half(grad_res)
    bias_out = jnp.sum(grad_res, axis=0, keepdims=True)
    rows_ref[:, 3 * D : 4 * D] = to_half(dot_tn(mix_rel_ref[...], res_half))
    mix_back = to_half(dot_nt(res_half, weights_ref[:, 3 * D : 4 * D]))
    grad_mix_ref[...] = to_half(dot_nn(mix_back, order))
    masks = pair_masks((ROWS, LANES))
    real = lax.broadcasted_iota(jnp.int32, (ROWS, ROWS), 1) < SEQ
    logs = log_ref[...]
    query_sums, value_sums = [], []
    for pair in range(HEADS // 2):
        cols = slice(pair * LANES, (pair + 1) * LANES)
        queries, keys, values = queries_ref[:, cols], keys_ref[:, cols], values_ref[:, cols]
        grad_mix = grad_mix_ref[:, cols]
        grad_q = jnp.zeros((ROWS, LANES), f32)
        grad_k = jnp.zeros((ROWS, LANES), f32)
        grad_v = jnp.zeros((ROWS, LANES), f32)
        for side in range(2):
            keys_one = only(masks[side], keys)
            log_total = jnp.sum(
                jnp.where(lane == 2 * pair + side, logs, 0.0), axis=-1, keepdims=True
            )
            probs = jnp.where(real, jnp.exp(dot_nt(queries, keys_one) - log_total), 0.0)
            grad_probs = dot_nt(grad_mix, only(masks[side], values))
            grad_scores = probs * (
                grad_probs - jnp.sum(probs * grad_probs, axis=-1, keepdims=True)
            )
            score_half = to_half(grad_scores)
            grad_q = grad_q + dot_nn(score_half, keys_one)
            grad_k = grad_k + dot_tn(score_half, only(masks[side], queries))
            grad_v = grad_v + dot_tn(to_half(probs), only(masks[side], grad_mix))
        grad_q = grad_q * HEAD ** (-0.5)
        proj_ref[:, cols] = to_half(grad_q)
        proj_ref[:, D + pair * LANES : D + (pair + 1) * LANES] = to_half(grad_k)
        proj_ref[:, 2 * D + pair * LANES : 2 * D + (pair + 1) * LANES] = to_half(grad_v)
        query_sums.append(jnp.sum(grad_q, axis=0, keepdims=True))
        value_sums.append(jnp.sum(grad_v, axis=0, keepdims=True))
    attn_rel = attn_rel_ref[...]
    for part in range(3):
        cols = slice(part * D, (part + 1) * D)
        rows_ref[:, cols] = to_half(dot_tn(attn_rel, proj_ref[:, cols]))
    attn_back = dot_nt(proj_ref[...], weights_ref[:, : 3 * D])
    grad_attn = lax.dot_general(
        attn_back,
        order.astype(f32),
        (((1,), (0,)), ((), ())),
        precision=EXACT,
        preferred_element_type=f32,
    )
    normed_one, inv_one = normalize(tokens_ref[...])
    gain_one = jnp.sum(grad_attn * normed_one, axis=0, keepdims=True)
    shift_one = jnp.sum(grad_attn, axis=0, keepdims=True)
    input_grad = grad_res + normalize_back(grad_attn * vec[0:1], normed_one, inv_one)
    input_ref[...] = input_grad[:SEQ]
    table = lax.broadcasted_iota(jnp.int32, (LANES, D), 0)
    vec_part = router_grad + bias_ref[...]
    small = [
        gain_one,
        shift_one,
        gain_two,
        shift_two,
        jnp.concatenate(query_sums, axis=1),
        jnp.concatenate(value_sums, axis=1),
        bias_out,
    ]
    for row, values in enumerate(small):
        vec_part = jnp.where(table == row, values, vec_part)
    rows_ref[:, 4 * D :] = to_half(dot_nt(order, to_half(vec_part)))


def whole_call(kernel, outs, scratch, flops, args):
    return pl.pallas_call(
        kernel,
        out_shape=[jax.ShapeDtypeStruct(shape, dtype) for shape, dtype in outs],
        in_specs=[pl.BlockSpec(memory_space=pltpu.VMEM)] * len(args),
        out_specs=[pl.BlockSpec(memory_space=pltpu.VMEM)] * len(outs),
        scratch_shapes=[pltpu.VMEM(shape, dtype) for shape, dtype in scratch],
        compiler_params=pltpu.CompilerParams(vmem_limit_bytes=VMEM_BYTES),
        cost_estimate=pl.CostEstimate(flops=flops, bytes_accessed=1 << 24, transcendentals=1 << 20),
    )(*args)


BIAS_PAIRS = [(i, (i % 2) * 4 + i // 2) for i in range(8)]


def body_column(
    tokens,
    cotangent,
    expert_ids,
    slot_pos,
    qkv_w,
    qkv_m,
    qkv_v,
    out_w,
    out_m,
    out_v,
    vectors,
    vec_m,
    vec_v,
    w_in,
    w_in_m,
    w_in_v,
    w_out,
    w_out_m,
    w_out_v,
    b_in,
    b_in_m,
    b_in_v,
):
    f32 = jnp.float32
    shard = jnp.concatenate(
        [
            to_half(qkv_w),
            to_half(out_w),
            jnp.pad(to_half(vectors.T), ((0, 0), (0, WIDE - 4 * D - vectors.shape[0]))),
        ],
        axis=1,
    )
    bias_in = lax.ppermute(to_half(b_in), COLUMN, BIAS_PAIRS)
    blocks = gather_line(shard)
    win_parts = host_parts(w_in)
    wout_parts = host_parts(w_out.T)
    blocks, win_parts, bias_in = after(blocks, win_parts, bias_in)
    bias_in = bias_in.astype(f32)
    win_parts = [to_host(part, turn) for turn, part in enumerate(win_parts)]
    first = jnp.concatenate(blocks[:2], axis=0)
    second = jnp.concatenate(blocks[2:], axis=0)
    first, second = join_swap(first, "x"), join_swap(second, "y")
    first, second = join_swap(first, "y"), join_swap(second, "x")
    first, second, win_parts[0] = after(first, second, win_parts[0])
    gathered = (
        first,
        lax.ppermute(first, "core", SWAP),
        second,
        lax.ppermute(second, "core", SWAP),
    )
    *gathered, win_parts[1] = after(*gathered, win_parts[1])

    pad = ((0, ROWS - SEQ), (0, 0))
    shared = (
        jnp.pad(tokens, pad),
        jnp.pad(cotangent, pad),
        *gathered,
        row_order(),
        jnp.pad(expert_ids, pad),
        jnp.pad(slot_pos, pad, constant_values=-1),
    )
    half = jnp.bfloat16
    *kept, sent = whole_call(
        attend_kernel,
        [((ROWS, D), half)] * 4
        + [((ROWS, LANES), f32), ((ROWS, D), half), ((ROWS, D), f32), ((ROWS, D), half)]
        + [((ROWS, LANES), f32), ((LANES, D), f32), ((LANES, D), f32)]
        + [((EXPERTS * CAP, 2 * D), half)],
        [((ROWS, D), half), ((D, WIDE), half)],
        6 << 30,
        shared,
    )
    sent, win_parts[2], wout_parts = after(sent, win_parts[2], wout_parts)
    wout_parts[0] = to_host(wout_parts[0], 0)

    def swap_chips(rows):
        chunks = rows.reshape(EXPERTS, -1, 2 * LANES)
        swapped = lax.all_to_all(chunks, CHIPS, split_axis=0, concat_axis=0, tiled=True)
        return swapped.reshape(rows.shape)

    routed_own = swap_chips(sent)
    routed_own, win_parts[3], wout_parts = after(routed_own, win_parts[3], wout_parts)
    wout_parts[1] = to_host(wout_parts[1], 1)
    routed = jnp.concatenate([routed_own, lax.ppermute(routed_own, "core", SWAP)], axis=0)
    rows_in, grads_in = routed[:, :D], routed[:, D:]

    weight_in = settle(win_parts)
    pre_act = jnp.dot(rows_in, weight_in, preferred_element_type=f32) + bias_in[None, :]
    activated, gelu_back = jax.vjp(jax.nn.gelu, pre_act)
    act_half = to_half(activated)
    act_half, wout_parts[2:] = after(act_half, wout_parts[2:])
    wout_parts[2:] = [to_host(wout_parts[turn], turn) for turn in (2, 3)]
    wout_back = owner_pieces(exact_dot(grads_in, act_half, ((0,), (0,))))
    weight_out = settle(wout_parts)
    expert_res = exact_dot(act_half, weight_out, ((1,), (1,)))
    grad_act = exact_dot(grads_in, weight_out, ((1,), (0,)))
    grad_pre = gelu_back(grad_act)[0]
    grad_bias_in = jnp.sum(grad_pre, axis=0)
    pre_half = to_half(grad_pre)
    grad_win = exact_dot(rows_in, pre_half, ((0,), (0,)))
    grad_slots = exact_dot(pre_half, weight_in, ((1,), (1,)))

    results = jnp.concatenate([expert_res, grad_slots], axis=1)
    there = lax.ppermute(to_half(results[EXPERTS * CAP :]), "core", SWAP)
    sent_back = to_half(results[: EXPERTS * CAP] + there)
    sent_back, wout_back[:2] = after(sent_back, wout_back[:2])
    wout_back[:2] = [to_owner(wout_back[turn], turn) for turn in (0, 1)]
    returned = swap_chips(sent_back)
    win_back = owner_pieces(grad_win)
    block_out, input_grad, rows = whole_call(
        retreat_kernel,
        [((SEQ, D), f32), ((SEQ, D), f32), ((D, WIDE), half)],
        [((ROWS, D), half), ((ROWS, 3 * D), half), ((D, WIDE), half)],
        12 << 30,
        (*shared, *kept, returned),
    )
    rows, wout_back, win_back = after(rows, wout_back, win_back)
    wout_back[2:] = [to_owner(wout_back[turn], turn) for turn in (2, 3)]
    win_back = [to_owner(piece, turn) for turn, piece in enumerate(win_back)]
    first, second = fold_swap(rows[: D // 2], rows[D // 2 :], "core", "core")
    w_out_grad = to_owners_end(wout_back).T
    w_out_all = (w_out_grad, *adamw_step(w_out, w_out_grad, w_out_m, w_out_v))
    first, second = fold_swap(first, second, "y", "x")
    first, second, win_back[0] = after(first, second, win_back[0])
    first, second = fold_swap(first, second, "x", "y")
    first, second, w_out_all, win_back[1:3], grad_bias_in = after(
        first, second, w_out_all, win_back[1:3], grad_bias_in
    )
    w_out_grad, w_out_new, w_out_m_new, w_out_v_new = w_out_all
    w_in_grad = to_owners_end(win_back)
    b_in_grad = lax.ppermute(grad_bias_in, COLUMN, [(host, owner) for owner, host in BIAS_PAIRS])
    blocks = [first[:SHARD], first[SHARD:], second[:SHARD], second[SHARD:]]
    summed = blocks[0].astype(f32)
    for step in (1, 2, 3):
        summed = summed + lax.ppermute(blocks[step], "group", shift_perm(-step)).astype(f32)
    qkv_grad = summed[:, : 3 * D]
    out_grad = summed[:, 3 * D : 4 * D]
    vec_grad = summed[:, 4 * D : 4 * D + vectors.shape[0]].T
    branch_bias_grad = jnp.concatenate([vec_grad[6:7], vec_grad[7 + EXPERTS :]], axis=0)
    qkv_new, qkv_m_new, qkv_v_new = adamw_step(qkv_w, qkv_grad, qkv_m, qkv_v)
    out_new, out_m_new, out_v_new = adamw_step(out_w, out_grad, out_m, out_v)
    vec_new, vec_m_new, vec_v_new = adamw_step(vectors, vec_grad, vec_m, vec_v)
    w_in_new, w_in_m_new, w_in_v_new = adamw_step(w_in, w_in_grad, w_in_m, w_in_v)
    b_in_new, b_in_m_new, b_in_v_new = adamw_step(b_in, b_in_grad, b_in_m, b_in_v)
    return (
        block_out,
        input_grad,
        qkv_grad,
        qkv_new,
        qkv_m_new,
        qkv_v_new,
        out_grad,
        out_new,
        out_m_new,
        out_v_new,
        vec_grad,
        vec_new,
        vec_m_new,
        vec_v_new,
        w_in_grad,
        w_in_new,
        w_in_m_new,
        w_in_v_new,
        w_out_grad,
        w_out_new,
        w_out_m_new,
        w_out_v_new,
        b_in_grad,
        b_in_new,
        b_in_m_new,
        b_in_v_new,
        branch_bias_grad,
    )


def solution(mesh):
    if mesh.shape["dp"] == 8 and mesh.shape["group"] == 4:
        inner = Mesh(mesh.devices.reshape(2, 2, 2, 4), AXES)
        body, dp, group, both = body_column, ("y", "x", "core"), "group", AXES
    else:
        inner, body, dp, group, both = mesh, body_any, "dp", "group", ("dp", "group")
    return jax.shard_map(
        body,
        mesh=inner,
        in_specs=(
            P(both, None),
            P(both, None),
            P(both, None),
            P(both, None),
            P(both, None),
            P(both, None),
            P(both, None),
            P(both, None),
            P(both, None),
            P(both, None),
            P(None, both),
            P(None, both),
            P(None, both),
            P(group, dp),
            P(group, dp),
            P(group, dp),
            P(dp, group),
            P(dp, group),
            P(dp, group),
            P(both),
            P(both),
            P(both),
        ),
        out_specs=(
            P(both, None),
            P(both, None),
            P(both, None),
            P(both, None),
            P(both, None),
            P(both, None),
            P(both, None),
            P(both, None),
            P(both, None),
            P(both, None),
            P(None, both),
            P(None, both),
            P(None, both),
            P(None, both),
            P(group, dp),
            P(group, dp),
            P(group, dp),
            P(group, dp),
            P(dp, group),
            P(dp, group),
            P(dp, group),
            P(dp, group),
            P(both),
            P(both),
            P(both),
            P(both),
            P(None, both),
        ),
        check_vma=False,
    )
```

```python
import jax
import jax.numpy as jnp
from jax import lax
from jax.experimental import pallas as pl
from jax.experimental.pallas import tpu as pltpu
from jax.sharding import Mesh, PartitionSpec as P

D = 768
HEADS = 12
HEAD = 64
FF = 3072
EXPERTS = 16
SEQ = 197
CAP = 25


LEARN_RATE = 0.15
BETA_ONE = 0.9
BETA_TWO = 0.999
ADAM_EPS = 1e-08
WEIGHT_DECAY = 0.1
CORR_ONE = 1.0 - BETA_ONE**2
CORR_TWO = 1.0 - BETA_TWO**2
NORM_EPS = 1e-06
EXACT = lax.Precision.HIGHEST


def to_half(values):
    return values.astype(jnp.bfloat16)


def heads_split(values):
    return values.reshape(-1, SEQ, HEADS, HEAD)


def normalize(values):
    average = jnp.mean(values, axis=-1, keepdims=True)
    centered = values - average
    inv_std = lax.rsqrt(jnp.mean(centered * centered, axis=-1, keepdims=True) + NORM_EPS)
    return (centered * inv_std, inv_std)


def normalize_back(grad_norm, normed, inv_std):
    return inv_std * (
        grad_norm
        - jnp.mean(grad_norm, axis=-1, keepdims=True)
        - normed * jnp.mean(grad_norm * normed, axis=-1, keepdims=True)
    )


def expert_table(ids_here):
    return (ids_here[..., None] == jnp.arange(EXPERTS)[None, None, :]).astype(jnp.float32)


def slot_table(ids_here, slots_here):
    kept_mask = slots_here >= 0
    target = ids_here * CAP + slots_here
    slot_hits = (target[..., None] == jnp.arange(EXPERTS * CAP)[None, None, :]) & kept_mask[
        ..., None
    ]
    return (slot_hits.astype(jnp.float32), kept_mask)


def select_rows(results, ids_here, slots_here):
    kept_mask = slots_here >= 0
    flat_index = jnp.where(kept_mask, ids_here * CAP + slots_here, 0)
    return (jnp.take(results, flat_index, axis=0), kept_mask)


def forward_rows(row_block, qkv_half, out_half, vec_real, router_half):
    normed_one, inv_one = normalize(row_block)
    attn_in = to_half(normed_one * vec_real[0] + vec_real[1])
    projected = jnp.dot(attn_in, qkv_half, preferred_element_type=jnp.float32)
    queries = to_half((projected[:, :D] + vec_real[4]) * HEAD ** (-0.5))
    keys_b = to_half(projected[:, D : 2 * D])
    values_b = to_half(projected[:, 2 * D :] + vec_real[5])
    scores = jnp.einsum(
        "ishd,ithd->ihst",
        heads_split(queries),
        heads_split(keys_b),
        preferred_element_type=jnp.float32,
    )
    log_total = jnp.log(jnp.sum(jnp.exp(scores), axis=-1))
    prob_half = to_half(jnp.exp(scores - log_total[..., None]))
    head_mix = to_half(
        jnp.einsum(
            "ihst,ithd->ishd", prob_half, heads_split(values_b), preferred_element_type=jnp.float32
        ).reshape(-1, D)
    )
    hidden_res = (
        row_block + jnp.dot(head_mix, out_half, preferred_element_type=jnp.float32) + vec_real[6]
    )
    normed_two, inv_two = normalize(hidden_res)
    moe_in = to_half(normed_two * vec_real[2] + vec_real[3])
    exp_logit = jnp.exp(
        jnp.einsum("td,ed->te", moe_in, router_half, preferred_element_type=jnp.float32)
    )
    route_prob = exp_logit / jnp.sum(exp_logit, axis=-1, keepdims=True)
    return (
        attn_in,
        normed_one,
        inv_one,
        queries,
        keys_b,
        values_b,
        log_total,
        head_mix,
        hidden_res,
        normed_two,
        inv_two,
        moe_in,
        route_prob,
    )


def backward_rows(
    saved, grad_moe, cot_rows, grad_gate, ids_here, qkv_half, out_half, vec_real, router_half
):
    (
        attn_in,
        normed_one,
        inv_one,
        queries,
        keys_b,
        values_b,
        log_total,
        head_mix,
        hidden_res,
        normed_two,
        inv_two,
        moe_in,
        route_prob,
    ) = saved
    onehot = expert_table(ids_here)
    grad_prob = jnp.sum(grad_gate[..., None] * onehot, axis=1)
    grad_logit = route_prob * (grad_prob - jnp.sum(route_prob * grad_prob, axis=-1, keepdims=True))
    logit_half = to_half(grad_logit)
    router_grad = jnp.einsum("te,td->ed", logit_half, moe_in, preferred_element_type=jnp.float32)
    grad_moe = grad_moe + jnp.dot(logit_half, router_half, preferred_element_type=jnp.float32)
    gain_two = jnp.sum(grad_moe * normed_two, axis=0)
    shift_two = jnp.sum(grad_moe, axis=0)
    grad_res = cot_rows + normalize_back(grad_moe * vec_real[2], normed_two, inv_two)
    res_half = to_half(grad_res)
    bias_out = jnp.sum(grad_res, axis=0)
    out_part = jnp.einsum("tf,td->fd", head_mix, res_half, preferred_element_type=jnp.float32)
    grad_mix = to_half(
        jnp.einsum("td,fd->tf", res_half, out_half, preferred_element_type=jnp.float32)
    )
    scores = jnp.einsum(
        "ishd,ithd->ihst",
        heads_split(queries),
        heads_split(keys_b),
        preferred_element_type=jnp.float32,
    )
    prob_full = jnp.exp(scores - log_total[..., None])
    prob_half = to_half(prob_full)
    grad_probs = jnp.einsum(
        "ishd,ithd->ihst",
        heads_split(grad_mix),
        heads_split(values_b),
        preferred_element_type=jnp.float32,
    )
    grad_values = jnp.einsum(
        "ihst,ishd->ithd", prob_half, heads_split(grad_mix), preferred_element_type=jnp.float32
    )
    grad_scores = prob_full * (grad_probs - jnp.sum(prob_full * grad_probs, axis=-1, keepdims=True))
    score_half = to_half(grad_scores)
    grad_queries = jnp.einsum(
        "ihst,ithd->ishd", score_half, heads_split(keys_b), preferred_element_type=jnp.float32
    ) * HEAD ** (-0.5)
    grad_keys = jnp.einsum(
        "ihst,ishd->ithd", score_half, heads_split(queries), preferred_element_type=jnp.float32
    )
    grad_queries = grad_queries.reshape(-1, D)
    grad_values = grad_values.reshape(-1, D)
    proj_half = to_half(
        jnp.concatenate([grad_queries, grad_keys.reshape(-1, D), grad_values], axis=1)
    )
    qkv_part = jnp.einsum("td,tq->dq", attn_in, proj_half, preferred_element_type=jnp.float32)
    grad_attn = jnp.einsum("tq,dq->td", proj_half, qkv_half, preferred_element_type=jnp.float32)
    gain_one = jnp.sum(grad_attn * normed_one, axis=0)
    shift_one = jnp.sum(grad_attn, axis=0)
    grad_rows = grad_res + normalize_back(grad_attn * vec_real[0], normed_one, inv_one)
    small_part = jnp.stack(
        [
            gain_one,
            shift_one,
            gain_two,
            shift_two,
            jnp.sum(grad_queries, axis=0),
            jnp.sum(grad_values, axis=0),
            bias_out,
        ]
    )
    return (grad_rows, qkv_part, out_part, small_part, router_grad)


def adamw_step(weight, grad, first_m, second_m):
    new_first = BETA_ONE * first_m + (1.0 - BETA_ONE) * grad
    new_second = BETA_TWO * second_m + (1.0 - BETA_TWO) * grad * grad
    step_dir = new_first / CORR_ONE / (jnp.sqrt(new_second / CORR_TWO) + ADAM_EPS)
    return (weight - LEARN_RATE * (step_dir + WEIGHT_DECAY * weight), new_first, new_second)


def body_any(
    tokens,
    cotangent,
    expert_ids,
    slot_pos,
    qkv_w,
    qkv_m,
    qkv_v,
    out_w,
    out_m,
    out_v,
    vectors,
    vec_m,
    vec_v,
    w_in,
    w_in_m,
    w_in_v,
    w_out,
    w_out_m,
    w_out_v,
    b_in,
    b_in_m,
    b_in_v,
):
    qkv_shard = to_half(qkv_w)
    out_shard = to_half(out_w)
    vec_shard = to_half(vectors)
    qkv_half, out_half, vec_half = (
        lax.all_gather(qkv_shard, ("dp", "group"), axis=0, tiled=True),
        lax.all_gather(out_shard, ("dp", "group"), axis=0, tiled=True),
        lax.all_gather(vec_shard, ("dp", "group"), axis=1, tiled=True),
    )
    win_full, wout_full, bin_full = (
        lax.all_gather(to_half(w_in), "group", axis=0, tiled=True),
        lax.all_gather(to_half(w_out), "group", axis=1, tiled=True),
        lax.all_gather(to_half(b_in), "group", axis=0, tiled=True),
    )
    vec_real = vec_half.astype(jnp.float32)
    router_half = vec_half[7 : 7 + EXPERTS]
    out_bias = vec_real[7 + EXPERTS :]
    hid_cols = win_full.shape[1]
    local_exp = max(1, hid_cols // FF)
    hid_width = hid_cols // local_exp
    split_count = FF // hid_width
    dp_count = lax.axis_size("dp")
    weight_in = win_full.reshape(D, local_exp, hid_width).transpose(1, 0, 2)
    weight_out = wout_full.reshape(local_exp, hid_width, D)
    bias_in = bin_full.astype(jnp.float32).reshape(local_exp, hid_width)

    def spread(buffer):
        return jnp.repeat(buffer.reshape(EXPERTS, CAP, D), split_count, axis=0)

    def to_experts(arrived):
        return (
            arrived.reshape(dp_count, local_exp, CAP, D)
            .transpose(1, 0, 2, 3)
            .reshape(local_exp, dp_count * CAP, D)
        )

    def to_sources(expert_rows):
        return (
            expert_rows.reshape(local_exp, dp_count, CAP, D)
            .transpose(1, 0, 2, 3)
            .reshape(dp_count * local_exp, CAP, D)
        )

    def join_parts(arrived):
        return jnp.sum(arrived.reshape(EXPERTS, split_count, CAP, D), axis=1).reshape(
            EXPERTS * CAP, D
        )

    saved = forward_rows(tokens, qkv_half, out_half, vec_real, router_half)
    slot_hits, kept_mask = slot_table(expert_ids, slot_pos)
    packed = to_half(
        jnp.einsum(
            "ts,td->sd",
            to_half(jnp.sum(slot_hits, axis=1)),
            saved[11],
            preferred_element_type=jnp.float32,
        )
    )
    routed_rows = to_experts(
        lax.all_to_all(spread(packed), "dp", split_axis=0, concat_axis=0, tiled=True)
    )
    pre_act = (
        jnp.einsum("erd,edh->erh", routed_rows, weight_in, preferred_element_type=jnp.float32)
        + bias_in[:, None, :]
    )
    expert_res = jnp.einsum(
        "erh,ehd->erd",
        to_half(jax.nn.gelu(pre_act)),
        weight_out,
        preferred_element_type=jnp.float32,
    )
    combined = join_parts(
        lax.all_to_all(
            to_sources(expert_res).astype(jnp.bfloat16),
            "dp",
            split_axis=0,
            concat_axis=0,
            tiled=True,
        ).astype(jnp.float32)
    )
    chosen, kept_mask = select_rows(combined, expert_ids, slot_pos)
    onehot = expert_table(expert_ids)
    chosen = chosen + jnp.einsum("tke,ed->tkd", onehot, out_bias, precision=EXACT)
    gate_vals = jnp.where(kept_mask, jnp.take_along_axis(saved[12], expert_ids, axis=1), 0.0)
    block_out = saved[8] + jnp.sum(gate_vals[..., None] * chosen, axis=1)
    grad_gate = jnp.where(kept_mask, jnp.sum(cotangent[:, None, :] * chosen, axis=-1), 0.0)
    weighted = gate_vals[..., None] * cotangent[:, None, :]
    grad_packed = to_half(jnp.einsum("tks,tkd->sd", slot_hits, weighted, precision=EXACT))
    bias_grad = jnp.einsum("tke,tkd->ed", onehot, weighted, precision=EXACT)
    grad_routed = to_experts(
        lax.all_to_all(spread(grad_packed), "dp", split_axis=0, concat_axis=0, tiled=True)
    )
    activated, gelu_back = jax.vjp(jax.nn.gelu, pre_act)
    act_half = to_half(activated)
    grad_act = jnp.einsum(
        "erd,ehd->erh", grad_routed, weight_out, preferred_element_type=jnp.float32
    )
    grad_wout = jnp.einsum(
        "erh,erd->ehd", act_half, grad_routed, preferred_element_type=jnp.float32
    )
    grad_pre = gelu_back(grad_act)[0]
    grad_bias_in = jnp.sum(grad_pre, axis=1)
    pre_half = to_half(grad_pre)
    grad_win = jnp.einsum("erd,erh->edh", routed_rows, pre_half, preferred_element_type=jnp.float32)
    grad_inputs = jnp.einsum(
        "erh,edh->erd", pre_half, weight_in, preferred_element_type=jnp.float32
    )
    slot_grads = join_parts(
        lax.all_to_all(
            to_sources(grad_inputs).astype(jnp.bfloat16),
            "dp",
            split_axis=0,
            concat_axis=0,
            tiled=True,
        ).astype(jnp.float32)
    )
    w_in_grad, w_out_grad, b_in_grad = (
        lax.psum_scatter(
            grad_win.transpose(1, 0, 2).reshape(D, hid_cols).astype(jnp.bfloat16),
            "group",
            scatter_dimension=0,
            tiled=True,
        ).astype(jnp.float32),
        lax.psum_scatter(
            grad_wout.reshape(hid_cols, D).astype(jnp.bfloat16),
            "group",
            scatter_dimension=1,
            tiled=True,
        ).astype(jnp.float32),
        lax.psum_scatter(
            grad_bias_in.reshape(hid_cols).astype(jnp.bfloat16),
            "group",
            scatter_dimension=0,
            tiled=True,
        ).astype(jnp.float32),
    )
    picked, kept_mask = select_rows(slot_grads, expert_ids, slot_pos)
    grad_moe = jnp.sum(jnp.where(kept_mask[..., None], picked, 0.0), axis=1)
    input_grad, qkv_part, out_part, small_part, router_grad = backward_rows(
        saved, grad_moe, cotangent, grad_gate, expert_ids, qkv_half, out_half, vec_real, router_half
    )
    vec_part = jnp.concatenate([small_part, router_grad, bias_grad], axis=0)
    qkv_grad, out_grad, vec_grad = (
        lax.psum_scatter(qkv_part, ("dp", "group"), scatter_dimension=0, tiled=True),
        lax.psum_scatter(out_part, ("dp", "group"), scatter_dimension=0, tiled=True),
        lax.psum_scatter(vec_part, ("dp", "group"), scatter_dimension=1, tiled=True),
    )
    branch_bias_grad = jnp.concatenate([vec_grad[6:7], vec_grad[7 + EXPERTS :]], axis=0)
    qkv_new, qkv_m_new, qkv_v_new = adamw_step(qkv_w, qkv_grad, qkv_m, qkv_v)
    out_new, out_m_new, out_v_new = adamw_step(out_w, out_grad, out_m, out_v)
    vec_new, vec_m_new, vec_v_new = adamw_step(vectors, vec_grad, vec_m, vec_v)
    w_in_new, w_in_m_new, w_in_v_new = adamw_step(w_in, w_in_grad, w_in_m, w_in_v)
    w_out_new, w_out_m_new, w_out_v_new = adamw_step(w_out, w_out_grad, w_out_m, w_out_v)
    b_in_new, b_in_m_new, b_in_v_new = adamw_step(b_in, b_in_grad, b_in_m, b_in_v)
    return (
        block_out,
        input_grad,
        qkv_grad,
        qkv_new,
        qkv_m_new,
        qkv_v_new,
        out_grad,
        out_new,
        out_m_new,
        out_v_new,
        vec_grad,
        vec_new,
        vec_m_new,
        vec_v_new,
        w_in_grad,
        w_in_new,
        w_in_m_new,
        w_in_v_new,
        w_out_grad,
        w_out_new,
        w_out_m_new,
        w_out_v_new,
        b_in_grad,
        b_in_new,
        b_in_m_new,
        b_in_v_new,
        branch_bias_grad,
    )


AXES = ("y", "x", "core", "group")
CHIPS = ("y", "x", "group")
COLUMN = ("core", "group")
SWAP = [(0, 1), (1, 0)]
WIDE = 3200
SHARD = 24


def exact_dot(left, right, dims):
    return lax.dot_general(left, right, (dims, ((), ())), preferred_element_type=jnp.float32)


def shift_perm(step):
    return [(i, (i + step) % 4) for i in range(4)]


def place():
    return tuple(lax.axis_index(name) for name in AXES)


def join_swap(rows, axis_name):
    return jnp.concatenate([rows, lax.ppermute(rows, axis_name, SWAP)], axis=0)


def gather_line(shard):
    return [shard] + [lax.ppermute(shard, "group", shift_perm(step)) for step in (1, 2, 3)]


def fold_swap(first, second, first_axis, second_axis):
    half = first.shape[0] // 2
    arrived = (
        lax.ppermute(first[half:], first_axis, SWAP),
        lax.ppermute(second[half:], second_axis, SWAP),
    )
    if first_axis != second_axis:
        arrived = after(*arrived)
    return [
        to_half(own[:half].astype(jnp.float32) + other.astype(jnp.float32))
        for own, other in zip((first, second), arrived)
    ]


def row_order():
    row_y, row_x, core, line = place()
    spot = jnp.arange(D)
    half = spot // 384
    other = (spot // 192) % 2
    outer = (spot // 96) % 2
    inner = (spot // 48) % 2
    step = half * 2 + (spot // SHARD) % 2
    y_rel = jnp.where(half == 0, outer, inner)
    x_rel = jnp.where(half == 0, inner, outer)
    owner = (((row_y ^ y_rel) * 2 + (row_x ^ x_rel)) * 2 + (core ^ other)) * 4 + (line - step) % 4
    feature = owner * SHARD + spot % SHARD
    return to_half(feature[:, None] == jnp.arange(D)[None, :])


def column_pairs(turn):
    pairs = []
    for core in range(2):
        for line in range(4):
            part = (line + turn) % 4
            pairs.append((core * 4 + line, (part % 2) * 4 + 2 * core + part // 2))
    return pairs


def host_parts(rows):
    row_y, row_x, core, line = place()
    width = rows.shape[1] // 4
    return [
        to_half(lax.dynamic_slice_in_dim(rows, (line + turn) % 4 * width, width, axis=1))
        for turn in range(4)
    ]


def to_host(part, turn):
    return lax.ppermute(part, COLUMN, column_pairs(turn))


def settle(arrived):
    row_y, row_x, core, line = place()
    stacked = jnp.stack(arrived, axis=0)
    here = 2 * (line % 2) + core
    pieces = [
        lax.dynamic_index_in_dim(stacked, (here - piece) % 4, axis=0, keepdims=False)
        for piece in range(4)
    ]
    return jnp.concatenate(pieces, axis=0)


def owner_pieces(grads):
    row_y, row_x, core, line = place()
    here = 2 * (line % 2) + core
    pieces = to_half(grads).reshape(4, -1, grads.shape[1])
    return [
        lax.dynamic_index_in_dim(pieces, (here - turn) % 4, axis=0, keepdims=False)
        for turn in range(4)
    ]


def to_owner(piece, turn):
    return lax.ppermute(piece, COLUMN, [(host, owner) for owner, host in column_pairs(turn)])


def after(gate, *values):
    return lax.optimization_barrier((gate, *values))


def to_owners_end(arrived):
    row_y, row_x, core, line = place()
    stacked = jnp.stack(arrived, axis=0)
    parts = [
        lax.dynamic_index_in_dim(stacked, (part - line) % 4, axis=0, keepdims=False)
        for part in range(4)
    ]
    return jnp.concatenate(parts, axis=1).astype(jnp.float32)


ROWS = 256
LANES = 128
VMEM_BYTES = 56 * 1024 * 1024


def pair_masks(shape):
    lane = lax.broadcasted_iota(jnp.int32, shape, 1)
    return lane < HEAD, lane >= HEAD


def dot_nt(left, right):
    return exact_dot(left, right, ((1,), (1,)))


def dot_nn(left, right):
    return exact_dot(left, right, ((1,), (0,)))


def dot_tn(left, right):
    return exact_dot(left, right, ((0,), (0,)))


def only(mask, values):
    return jnp.where(mask, values, jnp.zeros_like(values))


def slot_hit(target, count):
    return to_half(target == lax.broadcasted_iota(jnp.int32, (target.shape[0], count), 1))


def join_pieces(weights_ref, *pieces):
    rows = D // len(pieces)
    for index, piece in enumerate(pieces):
        weights_ref[index * rows : (index + 1) * rows, :] = piece[...]


def attend_kernel(
    tokens_ref,
    cot_ref,
    piece_one,
    piece_two,
    piece_three,
    piece_four,
    order_ref,
    ids_ref,
    slots_ref,
    attn_rel_ref,
    queries_ref,
    keys_ref,
    values_ref,
    log_ref,
    mix_rel_ref,
    hidden_ref,
    moe_ref,
    prob_ref,
    vec_ref,
    bias_ref,
    send_ref,
    mix_ref,
    weights_ref,
):
    f32 = jnp.float32
    join_pieces(weights_ref, piece_one, piece_two, piece_three, piece_four)
    order = order_ref[...]
    vec = dot_tn(weights_ref[:, 4 * D :], order)
    vec_ref[...] = vec
    tokens = tokens_ref[...]
    normed_one, inv_one = normalize(tokens)
    attn_in = to_half(normed_one * vec[0:1] + vec[1:2])
    attn_rel = to_half(dot_nt(attn_in, order))
    attn_rel_ref[...] = attn_rel
    queries_ref[...] = to_half(
        (dot_nn(attn_rel, weights_ref[:, :D]) + vec[4:5]) * HEAD ** (-0.5)
    )
    keys_ref[...] = to_half(dot_nn(attn_rel, weights_ref[:, D : 2 * D]))
    values_ref[...] = to_half(dot_nn(attn_rel, weights_ref[:, 2 * D : 3 * D]) + vec[5:6])
    masks = pair_masks((ROWS, LANES))
    real = lax.broadcasted_iota(jnp.int32, (ROWS, ROWS), 1) < SEQ
    lane = lax.broadcasted_iota(jnp.int32, (ROWS, LANES), 1)
    logs = jnp.zeros((ROWS, LANES), f32)
    for pair in range(HEADS // 2):
        cols = slice(pair * LANES, (pair + 1) * LANES)
        queries, keys, values = queries_ref[:, cols], keys_ref[:, cols], values_ref[:, cols]
        mixed = jnp.zeros((ROWS, LANES), f32)
        for side in range(2):
            scores = dot_nt(queries, only(masks[side], keys))
            powers = jnp.where(real, jnp.exp(scores), 0.0)
            log_total = jnp.log(jnp.sum(powers, axis=-1, keepdims=True))
            prob = jnp.where(real, jnp.exp(scores - log_total), 0.0)
            mixed = mixed + dot_nn(to_half(prob), only(masks[side], values))
            logs = jnp.where(lane == 2 * pair + side, log_total, logs)
        mix_ref[:, cols] = to_half(mixed)
    log_ref[...] = logs
    mix_rel = to_half(dot_nt(mix_ref[...], order))
    mix_rel_ref[...] = mix_rel
    hidden = tokens + dot_nn(mix_rel, weights_ref[:, 3 * D : 4 * D]) + vec[6:7]
    hidden_ref[...] = hidden
    normed_two, inv_two = normalize(hidden)
    moe_in = to_half(normed_two * vec[2:3] + vec[3:4])
    moe_ref[...] = moe_in
    logits = dot_nt(moe_in, to_half(vec))
    routed = (lane >= 7) & (lane < 7 + EXPERTS)
    exp_logit = jnp.where(routed, jnp.exp(jnp.where(routed, logits, 0.0)), 0.0)
    prob = exp_logit / jnp.sum(exp_logit, axis=-1, keepdims=True)
    prob_ref[...] = prob
    cot = cot_ref[...]
    hits, weighted, gates = [], [], jnp.zeros((ROWS, LANES), f32)
    for k in range(2):
        ids, slots = ids_ref[:, k : k + 1], slots_ref[:, k : k + 1]
        here = (lane == ids + 7) & (slots >= 0)
        gate = jnp.sum(jnp.where(here, prob, 0.0), axis=-1, keepdims=True)
        gates = gates + jnp.where(lane == ids + 7 + EXPERTS, gate, 0.0)
        hits.append(slot_hit(jnp.where(slots >= 0, ids * CAP + slots, -1), EXPERTS * CAP))
        weighted.append(to_half(gate * cot))
    bias_ref[...] = lax.dot_general(
        gates, cot, (((0,), (0,)), ((), ())), precision=EXACT, preferred_element_type=f32
    )
    send_ref[:, :D] = to_half(dot_tn(hits[0] + hits[1], moe_in))
    send_ref[:, D:] = to_half(dot_tn(hits[0], weighted[0]) + dot_tn(hits[1], weighted[1]))


def retreat_kernel(
    tokens_ref,
    cot_ref,
    piece_one,
    piece_two,
    piece_three,
    piece_four,
    order_ref,
    ids_ref,
    slots_ref,
    attn_rel_ref,
    queries_ref,
    keys_ref,
    values_ref,
    log_ref,
    mix_rel_ref,
    hidden_ref,
    moe_ref,
    prob_ref,
    vec_ref,
    bias_ref,
    returned_ref,
    block_ref,
    input_ref,
    rows_ref,
    grad_mix_ref,
    proj_ref,
    weights_ref,
):
    f32 = jnp.float32
    join_pieces(weights_ref, piece_one, piece_two, piece_three, piece_four)
    order = order_ref[...]
    vec = vec_ref[...]
    vec_half = to_half(vec)
    cot = cot_ref[...]
    hidden = hidden_ref[...]
    prob = prob_ref[...]
    lane = lax.broadcasted_iota(jnp.int32, (ROWS, LANES), 1)
    block_out = hidden
    grad_prob = jnp.zeros((ROWS, LANES), f32)
    grad_moe = jnp.zeros((ROWS, D), f32)
    for k in range(2):
        ids, slots = ids_ref[:, k : k + 1], slots_ref[:, k : k + 1]
        kept = slots >= 0
        mine = lane == ids + 7
        gate = jnp.sum(jnp.where(mine & kept, prob, 0.0), axis=-1, keepdims=True)
        hits = slot_hit(jnp.where(kept, ids * CAP + slots, -1), EXPERTS * CAP)
        bias_hit = to_half(lane == ids + 7 + EXPERTS)
        chosen = dot_nn(hits, returned_ref[:, :D]) + dot_nn(bias_hit, vec_half)
        block_out = block_out + gate * chosen
        grad_gate = jnp.where(kept, jnp.sum(cot * chosen, axis=-1, keepdims=True), 0.0)
        grad_prob = grad_prob + jnp.where(mine, grad_gate, 0.0)
        grad_moe = grad_moe + dot_nn(hits, returned_ref[:, D:])
    block_ref[...] = block_out[:SEQ]
    grad_logit = prob * (grad_prob - jnp.sum(prob * grad_prob, axis=-1, keepdims=True))
    logit_half = to_half(grad_logit)
    router_grad = dot_tn(logit_half, moe_ref[...])
    grad_moe = grad_moe + dot_nn(logit_half, vec_half)
    normed_two, inv_two = normalize(hidden)
    gain_two = jnp.sum(grad_moe * normed_two, axis=0, keepdims=True)
    shift_two = jnp.sum(grad_moe, axis=0, keepdims=True)
    grad_res = cot + normalize_back(grad_moe * vec[2:3], normed_two, inv_two)
    res_half = to_half(grad_res)
    bias_out = jnp.sum(grad_res, axis=0, keepdims=True)
    rows_ref[:, 3 * D : 4 * D] = to_half(dot_tn(mix_rel_ref[...], res_half))
    mix_back = to_half(dot_nt(res_half, weights_ref[:, 3 * D : 4 * D]))
    grad_mix_ref[...] = to_half(dot_nn(mix_back, order))
    masks = pair_masks((ROWS, LANES))
    real = lax.broadcasted_iota(jnp.int32, (ROWS, ROWS), 1) < SEQ
    logs = log_ref[...]
    query_sums, value_sums = [], []
    for pair in range(HEADS // 2):
        cols = slice(pair * LANES, (pair + 1) * LANES)
        queries, keys, values = queries_ref[:, cols], keys_ref[:, cols], values_ref[:, cols]
        grad_mix = grad_mix_ref[:, cols]
        grad_q = jnp.zeros((ROWS, LANES), f32)
        grad_k = jnp.zeros((ROWS, LANES), f32)
        grad_v = jnp.zeros((ROWS, LANES), f32)
        for side in range(2):
            keys_one = only(masks[side], keys)
            log_total = jnp.sum(
                jnp.where(lane == 2 * pair + side, logs, 0.0), axis=-1, keepdims=True
            )
            probs = jnp.where(real, jnp.exp(dot_nt(queries, keys_one) - log_total), 0.0)
            grad_probs = dot_nt(grad_mix, only(masks[side], values))
            grad_scores = probs * (
                grad_probs - jnp.sum(probs * grad_probs, axis=-1, keepdims=True)
            )
            score_half = to_half(grad_scores)
            grad_q = grad_q + dot_nn(score_half, keys_one)
            grad_k = grad_k + dot_tn(score_half, only(masks[side], queries))
            grad_v = grad_v + dot_tn(to_half(probs), only(masks[side], grad_mix))
        grad_q = grad_q * HEAD ** (-0.5)
        proj_ref[:, cols] = to_half(grad_q)
        proj_ref[:, D + pair * LANES : D + (pair + 1) * LANES] = to_half(grad_k)
        proj_ref[:, 2 * D + pair * LANES : 2 * D + (pair + 1) * LANES] = to_half(grad_v)
        query_sums.append(jnp.sum(grad_q, axis=0, keepdims=True))
        value_sums.append(jnp.sum(grad_v, axis=0, keepdims=True))
    attn_rel = attn_rel_ref[...]
    for part in range(3):
        cols = slice(part * D, (part + 1) * D)
        rows_ref[:, cols] = to_half(dot_tn(attn_rel, proj_ref[:, cols]))
    attn_back = dot_nt(proj_ref[...], weights_ref[:, : 3 * D])
    grad_attn = lax.dot_general(
        attn_back,
        order.astype(f32),
        (((1,), (0,)), ((), ())),
        precision=EXACT,
        preferred_element_type=f32,
    )
    normed_one, inv_one = normalize(tokens_ref[...])
    gain_one = jnp.sum(grad_attn * normed_one, axis=0, keepdims=True)
    shift_one = jnp.sum(grad_attn, axis=0, keepdims=True)
    input_grad = grad_res + normalize_back(grad_attn * vec[0:1], normed_one, inv_one)
    input_ref[...] = input_grad[:SEQ]
    table = lax.broadcasted_iota(jnp.int32, (LANES, D), 0)
    vec_part = router_grad + bias_ref[...]
    small = [
        gain_one,
        shift_one,
        gain_two,
        shift_two,
        jnp.concatenate(query_sums, axis=1),
        jnp.concatenate(value_sums, axis=1),
        bias_out,
    ]
    for row, values in enumerate(small):
        vec_part = jnp.where(table == row, values, vec_part)
    rows_ref[:, 4 * D :] = to_half(dot_nt(order, to_half(vec_part)))


def whole_call(kernel, outs, scratch, flops, args):
    return pl.pallas_call(
        kernel,
        out_shape=[jax.ShapeDtypeStruct(shape, dtype) for shape, dtype in outs],
        in_specs=[pl.BlockSpec(memory_space=pltpu.VMEM)] * len(args),
        out_specs=[pl.BlockSpec(memory_space=pltpu.VMEM)] * len(outs),
        scratch_shapes=[pltpu.VMEM(shape, dtype) for shape, dtype in scratch],
        compiler_params=pltpu.CompilerParams(vmem_limit_bytes=VMEM_BYTES),
        cost_estimate=pl.CostEstimate(flops=flops, bytes_accessed=1 << 24, transcendentals=1 << 20),
    )(*args)


BIAS_PAIRS = [(i, (i % 2) * 4 + i // 2) for i in range(8)]


def body_column(
    tokens,
    cotangent,
    expert_ids,
    slot_pos,
    qkv_w,
    qkv_m,
    qkv_v,
    out_w,
    out_m,
    out_v,
    vectors,
    vec_m,
    vec_v,
    w_in,
    w_in_m,
    w_in_v,
    w_out,
    w_out_m,
    w_out_v,
    b_in,
    b_in_m,
    b_in_v,
):
    f32 = jnp.float32
    shard = jnp.concatenate(
        [
            to_half(qkv_w),
            to_half(out_w),
            jnp.pad(to_half(vectors.T), ((0, 0), (0, WIDE - 4 * D - vectors.shape[0]))),
        ],
        axis=1,
    )
    bias_in = lax.ppermute(to_half(b_in), COLUMN, BIAS_PAIRS)
    blocks = gather_line(shard)
    win_parts = host_parts(w_in)
    wout_parts = host_parts(w_out.T)
    blocks, win_parts, bias_in = after(blocks, win_parts, bias_in)
    bias_in = bias_in.astype(f32)
    win_parts = [to_host(part, turn) for turn, part in enumerate(win_parts)]
    first = jnp.concatenate(blocks[:2], axis=0)
    second = jnp.concatenate(blocks[2:], axis=0)
    first, second = join_swap(first, "x"), join_swap(second, "y")
    first, second = join_swap(first, "y"), join_swap(second, "x")
    first, second, win_parts[0] = after(first, second, win_parts[0])
    gathered = (
        first,
        lax.ppermute(first, "core", SWAP),
        second,
        lax.ppermute(second, "core", SWAP),
    )
    *gathered, win_parts[1] = after(*gathered, win_parts[1])

    pad = ((0, ROWS - SEQ), (0, 0))
    shared = (
        jnp.pad(tokens, pad),
        jnp.pad(cotangent, pad),
        *gathered,
        row_order(),
        jnp.pad(expert_ids, pad),
        jnp.pad(slot_pos, pad, constant_values=-1),
    )
    half = jnp.bfloat16
    *kept, sent = whole_call(
        attend_kernel,
        [((ROWS, D), half)] * 4
        + [((ROWS, LANES), f32), ((ROWS, D), half), ((ROWS, D), f32), ((ROWS, D), half)]
        + [((ROWS, LANES), f32), ((LANES, D), f32), ((LANES, D), f32)]
        + [((EXPERTS * CAP, 2 * D), half)],
        [((ROWS, D), half), ((D, WIDE), half)],
        6 << 30,
        shared,
    )
    sent, win_parts[2], wout_parts = after(sent, win_parts[2], wout_parts)
    wout_parts[0] = to_host(wout_parts[0], 0)

    def swap_chips(rows):
        chunks = rows.reshape(EXPERTS, -1, 2 * LANES)
        swapped = lax.all_to_all(chunks, CHIPS, split_axis=0, concat_axis=0, tiled=True)
        return swapped.reshape(rows.shape)

    routed_own = swap_chips(sent)
    routed_own, win_parts[3], wout_parts = after(routed_own, win_parts[3], wout_parts)
    wout_parts[1] = to_host(wout_parts[1], 1)
    routed = jnp.concatenate([routed_own, lax.ppermute(routed_own, "core", SWAP)], axis=0)
    rows_in, grads_in = routed[:, :D], routed[:, D:]

    weight_in = settle(win_parts)
    pre_act = jnp.dot(rows_in, weight_in, preferred_element_type=f32) + bias_in[None, :]
    activated, gelu_back = jax.vjp(jax.nn.gelu, pre_act)
    act_half = to_half(activated)
    act_half, wout_parts[2:] = after(act_half, wout_parts[2:])
    wout_parts[2:] = [to_host(wout_parts[turn], turn) for turn in (2, 3)]
    wout_back = owner_pieces(exact_dot(grads_in, act_half, ((0,), (0,))))
    weight_out = settle(wout_parts)
    expert_res = exact_dot(act_half, weight_out, ((1,), (1,)))
    grad_act = exact_dot(grads_in, weight_out, ((1,), (0,)))
    grad_pre = gelu_back(grad_act)[0]
    grad_bias_in = jnp.sum(grad_pre, axis=0)
    pre_half = to_half(grad_pre)
    grad_win = exact_dot(rows_in, pre_half, ((0,), (0,)))
    grad_slots = exact_dot(pre_half, weight_in, ((1,), (1,)))

    results = jnp.concatenate([expert_res, grad_slots], axis=1)
    there = lax.ppermute(to_half(results[EXPERTS * CAP :]), "core", SWAP)
    sent_back = to_half(results[: EXPERTS * CAP] + there)
    sent_back, wout_back[:2] = after(sent_back, wout_back[:2])
    wout_back[:2] = [to_owner(wout_back[turn], turn) for turn in (0, 1)]
    returned = swap_chips(sent_back)
    win_back = owner_pieces(grad_win)
    block_out, input_grad, rows = whole_call(
        retreat_kernel,
        [((SEQ, D), f32), ((SEQ, D), f32), ((D, WIDE), half)],
        [((ROWS, D), half), ((ROWS, 3 * D), half), ((D, WIDE), half)],
        12 << 30,
        (*shared, *kept, returned),
    )
    rows, wout_back, win_back = after(rows, wout_back, win_back)
    wout_back[2:] = [to_owner(wout_back[turn], turn) for turn in (2, 3)]
    win_back = [to_owner(piece, turn) for turn, piece in enumerate(win_back)]
    first, second = fold_swap(rows[: D // 2], rows[D // 2 :], "core", "core")
    w_out_grad = to_owners_end(wout_back).T
    w_out_all = (w_out_grad, *adamw_step(w_out, w_out_grad, w_out_m, w_out_v))
    first, second = fold_swap(first, second, "y", "x")
    first, second, win_back[0] = after(first, second, win_back[0])
    first, second = fold_swap(first, second, "x", "y")
    first, second, w_out_all, win_back[1], grad_bias_in = after(
        first, second, w_out_all, win_back[1], grad_bias_in
    )
    w_out_grad, w_out_new, w_out_m_new, w_out_v_new = w_out_all
    w_in_grad = to_owners_end(win_back)
    b_in_grad = lax.ppermute(grad_bias_in, COLUMN, [(host, owner) for owner, host in BIAS_PAIRS])
    blocks = [first[:SHARD], first[SHARD:], second[:SHARD], second[SHARD:]]
    summed = blocks[0].astype(f32)
    for step in (1, 2, 3):
        summed = summed + lax.ppermute(blocks[step], "group", shift_perm(-step)).astype(f32)
    qkv_grad = summed[:, : 3 * D]
    out_grad = summed[:, 3 * D : 4 * D]
    vec_grad = summed[:, 4 * D : 4 * D + vectors.shape[0]].T
    branch_bias_grad = jnp.concatenate([vec_grad[6:7], vec_grad[7 + EXPERTS :]], axis=0)
    qkv_new, qkv_m_new, qkv_v_new = adamw_step(qkv_w, qkv_grad, qkv_m, qkv_v)
    out_new, out_m_new, out_v_new = adamw_step(out_w, out_grad, out_m, out_v)
    vec_new, vec_m_new, vec_v_new = adamw_step(vectors, vec_grad, vec_m, vec_v)
    w_in_new, w_in_m_new, w_in_v_new = adamw_step(w_in, w_in_grad, w_in_m, w_in_v)
    b_in_new, b_in_m_new, b_in_v_new = adamw_step(b_in, b_in_grad, b_in_m, b_in_v)
    return (
        block_out,
        input_grad,
        qkv_grad,
        qkv_new,
        qkv_m_new,
        qkv_v_new,
        out_grad,
        out_new,
        out_m_new,
        out_v_new,
        vec_grad,
        vec_new,
        vec_m_new,
        vec_v_new,
        w_in_grad,
        w_in_new,
        w_in_m_new,
        w_in_v_new,
        w_out_grad,
        w_out_new,
        w_out_m_new,
        w_out_v_new,
        b_in_grad,
        b_in_new,
        b_in_m_new,
        b_in_v_new,
        branch_bias_grad,
    )


def solution(mesh):
    if mesh.shape["dp"] == 8 and mesh.shape["group"] == 4:
        inner = Mesh(mesh.devices.reshape(2, 2, 2, 4), AXES)
        body, dp, group, both = body_column, ("y", "x", "core"), "group", AXES
    else:
        inner, body, dp, group, both = mesh, body_any, "dp", "group", ("dp", "group")
    return jax.shard_map(
        body,
        mesh=inner,
        in_specs=(
            P(both, None),
            P(both, None),
            P(both, None),
            P(both, None),
            P(both, None),
            P(both, None),
            P(both, None),
            P(both, None),
            P(both, None),
            P(both, None),
            P(None, both),
            P(None, both),
            P(None, both),
            P(group, dp),
            P(group, dp),
            P(group, dp),
            P(dp, group),
            P(dp, group),
            P(dp, group),
            P(both),
            P(both),
            P(both),
        ),
        out_specs=(
            P(both, None),
            P(both, None),
            P(both, None),
            P(both, None),
            P(both, None),
            P(both, None),
            P(both, None),
            P(both, None),
            P(both, None),
            P(both, None),
            P(None, both),
            P(None, both),
            P(None, both),
            P(None, both),
            P(group, dp),
            P(group, dp),
            P(group, dp),
            P(group, dp),
            P(dp, group),
            P(dp, group),
            P(dp, group),
            P(dp, group),
            P(both),
            P(both),
            P(both),
            P(both),
            P(None, both),
        ),
        check_vma=False,
    )
```
